32 devices in a mesh: rows: 2 (over y), cols: 8 (over z, x), fsdp: 2 (over core).
Axes of the slice: x: 2, y: 2, z: 4, core: 2. Of those that a mesh axis runs over, the one named last changes fastest.
Arguments:
- latent: bfloat16 [2, 2, 4, 128, 256], P(None, 'fsdp', None, 'rows', 'cols'), may hold values from -6 to 6
- time_embed: float32 [2, 2, 8, 4, 1024], P(None, 'fsdp', 'cols'), may hold values from -6 to 6
- image_rows: int32 [2, 2, 8, 4], P(None, 'fsdp', 'cols'), may hold values from 0 to 64, as said below
- pred_grad: bfloat16 [2, 2, 4, 128, 256], P(None, 'fsdp', None, 'rows', 'cols'), may hold values from -6 to 6
- embed_weight: bfloat16 [1536, 64], P(('rows', 'cols', 'fsdp')), may hold values from -0.75 to 0.75
- adaptive_weight: bfloat16 [1024, 7680], P(('rows', 'cols', 'fsdp')), may hold values from -0.1875 to 0.1875
- project_weight: bfloat16 [1536, 4608], P(('rows', 'cols', 'fsdp')), may hold values from -0.15625 to 0.15625
- output_weight: bfloat16 [1536, 1536], P(('rows', 'cols', 'fsdp')), may hold values from -0.15625 to 0.15625
- gate_up_weight: bfloat16 [1536, 8192], P(('rows', 'cols', 'fsdp')), may hold values from -0.15625 to 0.15625
- down_weight: bfloat16 [4096, 1536], P(('rows', 'cols', 'fsdp')), may hold values from -0.09375 to 0.09375
- final_weight: bfloat16 [1536, 64], P(('rows', 'cols', 'fsdp')), may hold values from -0.15625 to 0.15625
- norm_gains: bfloat16 [1536, 6], P(('rows', 'cols', 'fsdp')), may hold values from 0.25 to 1.75
Outputs:
- prediction: float32 [2, 2, 4, 128, 256], P(None, 'fsdp', None, 'rows', 'cols')
- latent_grad: float32 [2, 2, 4, 128, 256], P(None, 'fsdp', None, 'rows', 'cols')
- embed_grad: float32 [1536, 64], P(('rows', 'cols', 'fsdp'))
- adaptive_grad: float32 [1024, 7680], P(('rows', 'cols', 'fsdp'))
- project_grad: float32 [1536, 4608], P(('rows', 'cols', 'fsdp'))
- output_grad: float32 [1536, 1536], P(('rows', 'cols', 'fsdp'))
- gate_up_grad: float32 [1536, 8192], P(('rows', 'cols', 'fsdp'))
- down_grad: float32 [4096, 1536], P(('rows', 'cols', 'fsdp'))
- final_grad: float32 [1536, 64], P(('rows', 'cols', 'fsdp'))
- gain_grad: float32 [1536, 6], P(('rows', 'cols', 'fsdp'))
The draws below stay inside these ranges and needn't reach their ends.
Inputs may be any that keep to these rules, and one draw needn't show every extreme that they name: `image_rows`: each row of 4 heights sums to 64; in every micro-batch and group one column strip holds a single image of all 64 patch rows.
All inputs are finite; a program needn't handle non-finite values.
Results may differ from the reference program's by a relative error of at most 0.014.
Values may be sent and summed in bfloat16 or wider, within the bound.
No kernel may reach another device: no remote copies, remote signals or barrier semaphores. Data moves between devices by JAX's collectives and lax.ppermute only.
A program may use at most 512 MiB of HBM per device.

```python
import jax
import jax.numpy as jnp
from jax import lax

D = 1536
HEADS = 24
HD = 64
FF = 4096
TE = 1024
CHANNELS = 4
PIN = 64
IMGS = 4
MB = 2
PW = 16
SEQ_H = 64
SEQ_LEN = 1024
LH = 128
LW = 256
N_COLS = 8
N_FSDP = 2


def draw_image_rows(key, part):
    key = jax.random.fold_in(key, 11)
    cut_key, pick_key = jax.random.split(key)
    cut_rows = jax.random.randint(cut_key, (MB, N_FSDP, N_COLS, IMGS - 1), 0, SEQ_H + 1)
    cut_rows = jnp.sort(cut_rows, axis=-1)
    bottom_edge = jnp.zeros((MB, N_FSDP, N_COLS, 1), jnp.int32)
    top_edge = jnp.full((MB, N_FSDP, N_COLS, 1), SEQ_H, jnp.int32)
    boundaries = jnp.concatenate([bottom_edge, cut_rows.astype(jnp.int32), top_edge], axis=-1)
    heights = boundaries[..., 1:] - boundaries[..., :-1]
    whole_strip = jax.random.randint(pick_key, (MB, N_FSDP, 1), 0, N_COLS)
    chosen = jnp.arange(N_COLS, dtype=jnp.int32)[None, None, :] == whole_strip
    single = jnp.concatenate([jnp.full((1,), SEQ_H, jnp.int32), jnp.zeros((IMGS - 1,), jnp.int32)])
    return jnp.where(chosen[..., None], single[None, None, None, :], heights).astype(jnp.int32)


def shard_levels(rng, dims, shards, least, top_value):
    def one(position, blocks):
        draws = jax.random.uniform(jax.random.fold_in(jax.random.fold_in(rng, 6), position), (blocks,), jnp.float32, least / len(shards), top_value / len(shards))
        return jnp.repeat(jnp.exp(draws), dims[position] // blocks).reshape((-1,) + (1,) * (len(dims) - position - 1))

    level = one(*shards[0])
    for cut in shards[1:]:
        level = level * one(*cut)
    return level


def noise(key, shape, scale, most, cuts=(), kind=jnp.bfloat16):
    values = jax.random.normal(key, shape, jnp.float32) * scale
    if len(cuts) > 0:
        values = shard_levels(key, shape, cuts, -0.22, 0.18) * values
    return jnp.clip(values, min=-most, max=most).astype(kind)


def setup_inputs(seed: int = 0) -> dict:
    key_of = jax.random.split(jax.random.key(seed), 13)
    latent = noise(key_of[0], (MB, N_FSDP, CHANNELS, LH, LW), 1.0, 6.0, ((1, 2), (3, 2), (4, 8)))
    time_embed = noise(key_of[1], (MB, N_FSDP, N_COLS, IMGS, TE), 1.0, 6.0, ((1, 2), (2, 8)), jnp.float32)
    image_rows = draw_image_rows(jax.random.fold_in(key_of[12], 71), 0)
    pred_grad = noise(key_of[3], (MB, N_FSDP, CHANNELS, LH, LW), 1.0, 6.0, ((1, 2), (3, 2), (4, 8)))
    embed_weight = noise(key_of[4], (D, PIN), PIN ** -0.5, 0.75, ((0, 32),))
    adaptive_weight = noise(key_of[5], (TE, 5 * D), TE ** -0.5, 0.1875, ((0, 32),))
    project_weight = noise(key_of[6], (D, 3 * D), D ** -0.5, 0.15625, ((0, 32),))
    output_weight = noise(key_of[7], (D, D), D ** -0.5, 0.15625, ((0, 32),))
    gate_up_weight = noise(key_of[8], (D, 2 * FF), D ** -0.5, 0.15625, ((0, 32),))
    down_weight = noise(key_of[9], (FF, D), FF ** -0.5, 0.09375, ((0, 32),))
    final_weight = noise(key_of[10], (D, PIN), D ** -0.5, 0.15625, ((0, 32),))
    norm_gains = jnp.clip(1.0 + 0.15 * jax.random.normal(key_of[11], (D, 6), jnp.float32), 0.25, 1.75).astype(jnp.bfloat16)
    return dict(latent=latent, time_embed=time_embed, image_rows=image_rows, pred_grad=pred_grad, embed_weight=embed_weight, adaptive_weight=adaptive_weight, project_weight=project_weight, output_weight=output_weight, gate_up_weight=gate_up_weight, down_weight=down_weight, final_weight=final_weight, norm_gains=norm_gains)


epsilon = 1e-06
highest = lax.Precision.HIGHEST
negative = -1e+30

@jax.custom_vjp
def low(v):
    return lax.optimization_barrier(v.astype(jnp.bfloat16)).astype(jnp.float32)

@jax.custom_vjp
def low_back(v):
    return v

def low_keep(v):
    return (low(v), None)

def low_pass(kept, grad):
    return (grad,)

def back_keep(v):
    return (v, None)

def back_low(kept, grad):
    return (low(grad),)
low.defvjp(low_keep, low_pass)
low_back.defvjp(back_keep, back_low)

def matmul(left, right):
    return jnp.dot(left, right, precision=highest)

def rms_norm(values, gain):
    return values * lax.rsqrt(lax.optimization_barrier(jnp.mean(values * values, axis=-1, keepdims=True)) + epsilon) * gain

def layer_norm(values):
    centred = values - lax.optimization_barrier(jnp.mean(values, axis=-1, keepdims=True))
    return centred * lax.rsqrt(lax.optimization_barrier(jnp.mean(centred * centred, axis=-1, keepdims=True)) + epsilon)

def extract_patches(canvas):
    height = canvas.shape[1]
    width = canvas.shape[2]
    padded = jnp.pad(canvas, ((0, 0), (1, 1), (1, 1)))
    windows = [padded[:, a:a + height:2, b:b + width:2] for a in range(4) for b in range(4)]
    stacked = jnp.stack(windows, axis=1)
    return stacked.reshape(PIN, height // 2, width // 2).transpose(1, 2, 0)

def fold_patches(grid):
    padded_grid = jnp.pad(grid, ((1, 1), (1, 1), (0, 0)))
    outer_rows = padded_grid.shape[0]
    outer_cols = padded_grid.shape[1]
    pieces = padded_grid.reshape(outer_rows, outer_cols, CHANNELS, 4, 4)
    canvas = jnp.zeros((CHANNELS, 2 * outer_rows + 2, 2 * outer_cols + 2), jnp.float32)
    for a in range(4):
        for b in range(4):
            canvas = canvas.at[:, a:a + 2 * outer_rows:2, b:b + 2 * outer_cols:2].add(jnp.transpose(pieces[:, :, :, a, b], (2, 0, 1)))
    return canvas[:, 3:2 * outer_rows - 1, 3:2 * outer_cols - 1]

def strip_layout(heights):
    starts = (jnp.cumsum(heights) - heights).astype(jnp.int32)
    rows_all = jnp.arange(SEQ_H, dtype=jnp.int32)
    image_of = lax.optimization_barrier(jnp.sum((rows_all[:, None] >= starts[None, 1:]).astype(jnp.int32), axis=1)).astype(jnp.int32)
    start_of = lax.optimization_barrier(jnp.sum(jnp.where(image_of[:, None] == jnp.arange(IMGS, dtype=jnp.int32)[None, :], starts[None, :], 0), axis=1)).astype(jnp.int32)
    return (image_of, (rows_all - start_of).astype(jnp.int32))

def rope_tables(row_place, column):
    quarter = HD // 4
    frequency = 10000.0 ** (-jnp.arange(quarter, dtype=jnp.float32) / quarter)
    row_angle = row_place.astype(jnp.float32)[:, None] * frequency[None, :]
    col_angle = column.astype(jnp.float32)[:, None] * frequency[None, :]
    angles = jnp.concatenate([row_angle, row_angle, col_angle, col_angle], axis=1)
    return (jnp.cos(angles), jnp.sin(angles))

def rotate(values, cosine, sine_table):
    tok_count = values.shape[0]
    split = values.reshape(tok_count, HEADS, 2, 2, HD // 4)
    swapped = jnp.stack([-split[:, :, :, 1, :], split[:, :, :, 0, :]], axis=3).reshape(tok_count, HEADS, HD)
    plain = values.reshape(tok_count, HEADS, HD)
    return (plain * cosine[:, None, :] + swapped * sine_table[:, None, :]).reshape(tok_count, D)

def strip_attention(queries, keys, values, image_of):
    length = queries.shape[0]
    block_rows = min(512, length)
    score_scale = HD ** (-0.5)
    q_heads = queries.reshape(length // block_rows, block_rows, HEADS, HD)
    k_heads = keys.reshape(length, HEADS, HD)
    v_heads = values.reshape(length, HEADS, HD)

    def one_block(inputs):
        q_block, block_image = inputs
        scores = low_back(jnp.einsum('qhd,khd->hqk', q_block, k_heads, precision=highest) * score_scale)
        same_image = block_image[:, None] == image_of[None, :]
        scores = jnp.where(same_image[None], scores, negative)
        row_top = lax.optimization_barrier(jnp.max(scores, axis=-1, keepdims=True))
        raised = jnp.exp(scores - row_top)
        chances = low(raised / lax.optimization_barrier(jnp.sum(raised, axis=-1, keepdims=True)))
        return jnp.einsum('hqk,khd->qhd', chances, v_heads, precision=highest).reshape(block_rows, D)
    blocks = lax.map(jax.checkpoint(one_block), (q_heads, image_of.reshape(-1, block_rows)))
    return blocks.reshape(length, D)

def strip_forward(weights, patch_rows, temb_rows, heights):
    w_embed, w_adaptive, w_project, w_output, w_gate_up, w_down, w_final, gain_cols = weights
    image_of, place_of = strip_layout(heights)
    token_image = jnp.repeat(image_of, PW)
    token_place = jnp.repeat(place_of, PW)
    token_column = jnp.tile(jnp.arange(PW, dtype=jnp.int32), SEQ_H)
    embedded = low_back(matmul(patch_rows, w_embed.T))
    condition = low(jax.nn.silu(temb_rows))
    per_image = matmul(condition, w_adaptive)
    modulation = jnp.take(per_image, token_image, axis=0)
    scale_attn = modulation[:, 0:D]
    gate_attn = modulation[:, D:2 * D]
    scale_ffn = modulation[:, 2 * D:3 * D]
    gate_ffn = modulation[:, 3 * D:4 * D]
    scale_out = modulation[:, 4 * D:5 * D]
    normed = low(rms_norm(embedded, gain_cols[:, 0]) * (1.0 + scale_attn))
    projected = low_back(matmul(normed, w_project))
    cosine, sine_table = rope_tables(token_place, token_column)
    queries = low_back(low(rotate(rms_norm(projected[:, :D], gain_cols[:, 1]), cosine, sine_table)))
    keys = low_back(low(rotate(rms_norm(projected[:, D:2 * D], gain_cols[:, 2]), cosine, sine_table)))
    values = low_back(low(projected[:, 2 * D:]))
    attended = low_back(low(strip_attention(queries, keys, values, token_image)))
    attn_out = low_back(matmul(attended, w_output))
    mixed = embedded + jnp.tanh(gate_attn) * rms_norm(attn_out, gain_cols[:, 3])
    normed_ffn = low(rms_norm(mixed, gain_cols[:, 4]) * (1.0 + scale_ffn))
    gate_up = low_back(matmul(normed_ffn, w_gate_up))
    hidden = low(jax.nn.silu(gate_up[:, :FF]) * gate_up[:, FF:])
    ffn_out = low_back(matmul(hidden, w_down))
    final_state = mixed + jnp.tanh(gate_ffn) * rms_norm(ffn_out, gain_cols[:, 5])
    final_normed = low(layer_norm(final_state) * (1.0 + scale_out))
    return low(matmul(final_normed, w_final))

def canvas_forward(weights, canvas, temb_rows, heights):
    patches = low_back(extract_patches(canvas))
    strips = patches.reshape(SEQ_H, N_COLS, PW, PIN).transpose(1, 0, 2, 3).reshape(N_COLS, SEQ_LEN, PIN)

    def step(carry, inputs):
        return (carry, strip_forward(weights, inputs[0], inputs[1], inputs[2]))
    pieces = lax.scan(jax.checkpoint(step), jnp.zeros((), jnp.float32), (strips, temb_rows, heights))[1]
    grid = pieces.reshape(N_COLS, SEQ_H, PW, PIN).transpose(1, 0, 2, 3).reshape(SEQ_H, N_COLS * PW, PIN)
    return fold_patches(grid)

def reference(latent, time_embed, image_rows, pred_grad, embed_weight, adaptive_weight, project_weight, output_weight, gate_up_weight, down_weight, final_weight, norm_gains):
    weights = (embed_weight.astype(jnp.float32), adaptive_weight.astype(jnp.float32), project_weight.astype(jnp.float32), output_weight.astype(jnp.float32), gate_up_weight.astype(jnp.float32), down_weight.astype(jnp.float32), final_weight.astype(jnp.float32), norm_gains.astype(jnp.float32))
    canvases = latent.astype(jnp.float32).reshape(MB * N_FSDP, CHANNELS, LH, LW)
    temb_all = time_embed.reshape(MB * N_FSDP, N_COLS, IMGS, TE)
    heights_all = image_rows.reshape(MB * N_FSDP, N_COLS, IMGS)

    def forward(canvas_all, weight_all):

        def step(carry, inputs):
            return (carry, canvas_forward(weight_all, inputs[0], inputs[1], inputs[2]))
        return lax.scan(jax.checkpoint(step), jnp.zeros((), jnp.float32), (canvas_all, temb_all, heights_all))[1]
    predicted, pullback = jax.vjp(forward, canvases, weights)
    grad_canvas, grad_weights = pullback(pred_grad.astype(jnp.float32).reshape(predicted.shape))
    return (predicted.reshape(latent.shape), grad_canvas.reshape(latent.shape), grad_weights[0], grad_weights[1], grad_weights[2], grad_weights[3], grad_weights[4], grad_weights[5], grad_weights[6], grad_weights[7])
```

```python
from functools import partial

import jax
import jax.numpy as jnp
from jax import lax
from jax.experimental import pallas as pl
from jax.experimental.pallas import tpu as pltpu
from jax.sharding import PartitionSpec as P

D = 1536
HEADS = 24
HD = 64
FF = 4096
CHANNELS = 4
PIN = 64
IMGS = 4
CELL = 16
LANES = 128
ALL = ("rows", "cols", "fsdp")

epsilon = 1e-06
highest = lax.Precision.HIGHEST
mask_level = 256.0
f32 = jnp.float32
bf16 = jnp.bfloat16
vmem_bytes = 60 * 1024 * 1024


def dot_nn(left, right):
    return lax.dot_general(left, right, (((1,), (0,)), ((), ())), preferred_element_type=f32)


def dot_nt(left, right):
    return lax.dot_general(left, right, (((1,), (1,)), ((), ())), preferred_element_type=f32)


def dot_tn(left, right):
    return lax.dot_general(left, right, (((0,), (0,)), ((), ())), preferred_element_type=f32)


def row_mean(values):
    return jnp.mean(values, axis=-1, keepdims=True)


def inverse_rms(values):
    return lax.rsqrt(row_mean(values * values) + epsilon)


def whole(shape):
    zeros = (0,) * len(shape)
    return pl.BlockSpec(shape, lambda i: zeros, pipeline_mode=pl.Buffered(1))


def picked(image, table):
    choice = table[IMGS - 1 : IMGS, :]
    for index in range(IMGS - 2, -1, -1):
        choice = jnp.where(image == index, table[index : index + 1, :], choice)
    return choice


def image_sums(onehot, product):
    upper = product.astype(bf16)
    lower = (product - upper.astype(f32)).astype(bf16)
    return dot_nn(onehot, upper) + dot_nn(onehot, lower)


def matmul_rows(
    name, lefts, weight, kind, tile, row_ins, consts, row_outs, sum_rows, chunk_body,
    before=None, after=None, block_scratch=(), flops=0,
):
    tokens = lefts[0].shape[0]
    width = weight.shape[1] if kind == "nn" else weight.shape[0]
    depth = weight.shape[0] if kind == "nn" else weight.shape[1]
    block = min(256, tokens)
    chunk = 32
    tiles = width // tile
    blocks = tokens // block
    counts = (len(lefts), len(row_ins), len(consts), len(row_outs), len(sum_rows))

    def kernel(*refs):
        refs = list(refs)
        take = lambda n: [refs.pop(0) for _ in range(n)]
        left_refs = take(counts[0])
        weight_ref = take(1)[0]
        in_refs, const_refs = take(counts[1]), take(counts[2])
        out_refs, sum_refs = take(counts[3]), take(counts[4])
        total = refs.pop(0)
        scratch = refs
        step = pl.program_id(0)

        @pl.when(step < tiles)
        def _():
            offset = 0
            value = None
            for left in left_refs:
                size = left.shape[1]
                if kind == "nn":
                    term = dot_nn(left[...], weight_ref[offset : offset + size, :])
                else:
                    term = dot_nt(left[...], weight_ref[:, offset : offset + size])
                value = term if value is None else value + term
                offset += size
            total[:, pl.ds(pl.multiple_of(step * tile, tile), tile)] = value

        @pl.when(step == tiles)
        def _():
            for ref in sum_refs:
                ref[...] = jnp.zeros_like(ref)

        @pl.when(step >= tiles)
        def _():
            start = pl.multiple_of((step - tiles) * block, block)
            if before is not None:
                before(in_refs, const_refs, out_refs, scratch)

            def one(index, carry):
                low = pl.multiple_of(index * chunk, chunk)
                rows = pl.ds(low, chunk)
                chunk_body(
                    total[pl.ds(pl.multiple_of(start + low, chunk), chunk), :],
                    rows, in_refs, const_refs, out_refs, scratch,
                )
                return carry

            lax.fori_loop(0, block // chunk, one, 0)
            if after is not None:
                after(in_refs, const_refs, out_refs, sum_refs, scratch)

    def row_map(i):
        return (jnp.maximum(i - tiles, 0), 0)

    def col_map(i):
        return (0, jnp.maximum(i - tiles, 0))

    weight_shape = (depth, tile) if kind == "nn" else (tile, depth)
    if kind == "nn":
        weight_spec = pl.BlockSpec(weight_shape, lambda i: (0, jnp.minimum(i, tiles - 1)))
    else:
        weight_spec = pl.BlockSpec(weight_shape, lambda i: (jnp.minimum(i, tiles - 1), 0))
    in_specs = [whole(left.shape) for left in lefts] + [weight_spec]
    for array in row_ins:
        if array.shape[0] == tokens:
            in_specs.append(pl.BlockSpec((block, array.shape[1]), row_map))
        else:
            in_specs.append(pl.BlockSpec((array.shape[0], block), col_map))
    in_specs += [whole(array.shape) for array in consts]
    out_specs = [pl.BlockSpec((block, cols), row_map) for cols, _ in row_outs]
    out_specs += [pl.BlockSpec((count, width), lambda i: (0, 0)) for count in sum_rows]
    out_shape = [jax.ShapeDtypeStruct((tokens, cols), kind_) for cols, kind_ in row_outs]
    out_shape += [jax.ShapeDtypeStruct((count, width), f32) for count in sum_rows]
    return pl.pallas_call(
        kernel,
        grid=(tiles + blocks,),
        in_specs=in_specs,
        out_specs=out_specs,
        out_shape=out_shape,
        scratch_shapes=[pltpu.VMEM((tokens, width), f32)]
        + [pltpu.VMEM((block, cols), kind_) for cols, kind_ in block_scratch],
        compiler_params=pltpu.CompilerParams(vmem_limit_bytes=vmem_bytes),
        cost_estimate=pl.CostEstimate(
            flops=2 * tokens * width * depth,
            bytes_accessed=2 * (width * depth + tokens * depth) + 8 * tokens * width,
            transcendentals=0,
        ),
        name=name,
    )(*lefts, weight, *row_ins, *consts)


def swapped(values, first):
    return jnp.where(first, pltpu.roll(values, LANES - 16, 1), pltpu.roll(values, 16, 1))


def first_lanes(rows):
    lane = lax.broadcasted_iota(jnp.int32, (rows, LANES), 1)
    return lax.rem(lane, 32) < 16


def project_rows(patches, image, cosine, sine, w_embed, pre_table, weights, gains, place):
    tokens = patches.shape[0]
    chunk = 32
    tile = 256
    blocks = D // tile
    pieces = place is not None
    count = len(weights)
    share = 0 if not pieces else D // len(place[1][0])

    def kernel(*refs):
        refs = list(refs)
        patches_ref, image_ref, cos_ref, sin_ref, embed_ref, pre_ref, gain_ref = refs[:7]
        weight_refs = refs[7 : 7 + count]
        rest = refs[7 + count :]
        if pieces:
            me_ref, embedded_ref, normed_ref, out_ref, hat_ref, inverse_ref = rest[:6]
            weight_ref, total, sems = rest[6:]
        else:
            embedded_ref, normed_ref, out_ref, hat_ref, inverse_ref, total = rest
            weight_ref = weight_refs[0]
        step = pl.program_id(0)

        def copies(part):
            half = len(place[1][part]) // 2
            listed = []
            for index, mask in enumerate(place[1][part]):
                low = pl.multiple_of((me_ref[0] ^ mask) * share, share)
                source = weight_refs[2 * part + index // half]
                listed.append(
                    pltpu.make_async_copy(
                        source.at[pl.ds((index % half) * share, share), :],
                        weight_ref.at[pl.ds(low, share), :],
                        sems.at[index],
                    )
                )
            return listed

        if pieces:
            for part in range(3):

                @pl.when(step == part)
                def _():
                    for copy in copies(part):
                        copy.start()

        @pl.when(step == 0)
        def _():
            total[...] = dot_nt(patches_ref[...], embed_ref[...])

            def one(index, carry):
                rows = pl.ds(pl.multiple_of(index * chunk, chunk), chunk)
                value = total[rows, :]
                embedded_ref[rows, :] = value
                normed_ref[rows, :] = (
                    value * inverse_rms(value) * picked(image_ref[rows, :1], pre_ref[...])
                ).astype(bf16)
                return carry

            lax.fori_loop(0, tokens // chunk, one, 0)

        if pieces:
            for part in range(3):

                @pl.when(step == part)
                def _():
                    for copy in copies(part):
                        copy.wait()

        for index in range(blocks):
            cols = slice(index * tile, (index + 1) * tile)
            total[:, cols] = dot_nn(normed_ref[...], weight_ref[:, cols])

        @pl.when(step < 2)
        def _():
            gain = gain_ref[pl.ds(step, 1), :]

            def one(index, carry):
                rows = pl.ds(pl.multiple_of(index * chunk, chunk), chunk)
                value = total[rows, :]
                inverse = inverse_rms(value)
                hat = value * inverse
                hat_ref[rows, :] = hat.astype(bf16)
                inverse_ref[rows, :] = jnp.broadcast_to(inverse, (chunk, LANES))
                scaled = hat * gain
                first = first_lanes(chunk)
                cos_rows = cos_ref[rows, :]
                sin_rows = sin_ref[rows, :]
                for lane in range(0, D, LANES):
                    part = scaled[:, lane : lane + LANES]
                    turned = part * cos_rows + swapped(part, first) * sin_rows
                    out_ref[rows, lane : lane + LANES] = turned.astype(bf16)
                return carry

            lax.fori_loop(0, tokens // chunk, one, 0)

        @pl.when(step == 2)
        def _():
            out_ref[...] = total[...].astype(bf16)

    weight_specs = [pl.BlockSpec((D, D), lambda i: (0, i))]
    if pieces:
        weight_specs = [pl.BlockSpec(memory_space=pl.ANY)] * count
        weight_specs.append(pl.BlockSpec(memory_space=pltpu.SMEM))
        weights = list(weights) + [place[0]]
    out_specs = [
        pl.BlockSpec((tokens, D), lambda i: (0, 0), pipeline_mode=pl.Buffered(1)),
        pl.BlockSpec((tokens, D), lambda i: (0, 0), pipeline_mode=pl.Buffered(1)),
        pl.BlockSpec((tokens, D), lambda i: (0, i)),
        pl.BlockSpec((tokens, D), lambda i: (0, jnp.minimum(i, 1))),
        pl.BlockSpec((tokens, LANES), lambda i: (0, jnp.minimum(i, 1))),
    ]
    out_shape = [
        jax.ShapeDtypeStruct((tokens, D), f32),
        jax.ShapeDtypeStruct((tokens, D), bf16),
        jax.ShapeDtypeStruct((tokens, 3 * D), bf16),
        jax.ShapeDtypeStruct((tokens, 2 * D), bf16),
        jax.ShapeDtypeStruct((tokens, 2 * LANES), f32),
    ]
    scratch = [pltpu.VMEM((tokens, D), f32)]
    if pieces:
        out_specs.append(pl.BlockSpec((D, D), lambda i: (0, i)))
        out_shape.append(jax.ShapeDtypeStruct((D, 3 * D), bf16))
        scratch.append(pltpu.SemaphoreType.DMA((len(place[1][0]),)))
    results = pl.pallas_call(
        kernel,
        grid=(3,),
        in_specs=[
            whole(patches.shape),
            whole(image.shape),
            whole(cosine.shape),
            whole(sine.shape),
            whole(w_embed.shape),
            whole(pre_table.shape),
            whole(gains.shape),
        ]
        + weight_specs,
        out_specs=out_specs,
        out_shape=out_shape,
        scratch_shapes=scratch,
        compiler_params=pltpu.CompilerParams(vmem_limit_bytes=vmem_bytes),
        cost_estimate=pl.CostEstimate(
            flops=6 * tokens * D * D, bytes_accessed=6 * D * D + 24 * tokens * D, transcendentals=0
        ),
        name="project_rows",
    )(patches, image, cosine, sine, w_embed, pre_table, gains, *weights)
    return list(results) + ([] if pieces else [weights[0]])


def attention_grads(which, normed, project_back, attended, attn_back, place):
    tokens = normed.shape[0]
    tile = 256
    tiles = D // tile
    side = D // 3
    masks = place[1][which]
    share = D // len(masks)

    def kernel(left_ref, back_ref, other_ref, attn_ref, me_ref, out_ref, held, sems):
        step = pl.program_id(0)
        rows = pl.ds(pl.multiple_of(step * tile, tile), tile)
        held[rows, :D] = dot_tn(left_ref[...], back_ref[...]).astype(bf16)
        held[rows, D:] = dot_tn(other_ref[...], attn_ref[...]).astype(bf16)

        @pl.when(step == tiles - 1)
        def _():
            listed = []
            for index, mask in enumerate(masks):
                low = pl.multiple_of((me_ref[0] ^ mask) * share, share)
                listed.append(
                    pltpu.make_async_copy(
                        held.at[pl.ds(low, share), :],
                        out_ref.at[pl.ds(index * share, share), :],
                        sems.at[index],
                    )
                )
            for copy in listed:
                copy.start()
            for copy in listed:
                copy.wait()

    return pl.pallas_call(
        kernel,
        grid=(tiles,),
        in_specs=[
            pl.BlockSpec((tokens, tile), lambda i: (0, i)),
            pl.BlockSpec((tokens, D), lambda i: (0, which), pipeline_mode=pl.Buffered(1)),
            pl.BlockSpec((tokens, tile), lambda i: (0, i)),
            pl.BlockSpec((tokens, side), lambda i: (0, which), pipeline_mode=pl.Buffered(1)),
            pl.BlockSpec(memory_space=pltpu.SMEM),
        ],
        out_specs=pl.BlockSpec(memory_space=pl.ANY),
        out_shape=jax.ShapeDtypeStruct((D, D + side), bf16),
        scratch_shapes=[
            pltpu.VMEM((D, D + side), bf16),
            pltpu.SemaphoreType.DMA((len(masks),)),
        ],
        compiler_params=pltpu.CompilerParams(vmem_limit_bytes=vmem_bytes),
        cost_estimate=pl.CostEstimate(
            flops=2 * tokens * D * (D + side),
            bytes_accessed=2 * D * (D + side) + 8 * tokens * D,
            transcendentals=0,
        ),
        name="attention_grads",
    )(normed, project_back, attended, attn_back, place[0])


def head_lanes(shape, axis, head):
    lane = lax.broadcasted_iota(jnp.int32, shape, axis)
    return (lane >= HD) == (head == 1)


def attend(queries, keys, values, spec_of, width, query_image, key_image):
    length = queries.shape[0]
    pairs = width // LANES
    part = min(256, length)

    def kernel(q_ref, k_ref, v_ref, qi_ref, ki_ref, out_ref, log_ref):
        key_block = k_ref[...]
        value_turned = v_ref[...].T
        key_parts = []
        value_parts = []
        for head in range(2):
            mine = head_lanes((length, LANES), 1, head)
            key_parts.append(jnp.where(mine, key_block, ki_ref[...]))
            value_parts.append(
                jnp.where(head_lanes((LANES, length), 0, head), value_turned, jnp.ones((), bf16))
            )

        def one(index, carry):
            rows = pl.ds(pl.multiple_of(index * part, part), part)
            query = q_ref[rows, :] * jnp.asarray(HD ** (-0.5), bf16)
            turned = []
            for head in range(2):
                mine = head_lanes((part, LANES), 1, head)
                scores = dot_nt(key_parts[head], jnp.where(mine, query, qi_ref[rows, :]))
                top = jnp.max(scores, axis=0, keepdims=True)
                raised = jnp.exp(scores - top).astype(bf16)
                result = dot_nn(value_parts[head], raised)
                lane = HD * (1 - head)
                count = result[lane : lane + 1, :]
                turned.append(result[head * HD : (head + 1) * HD, :] / count)
                log_ref[0, pl.ds(head, 1), rows] = top + jnp.log(count)
            out_ref[rows, :] = jnp.concatenate(turned, axis=0).T.astype(bf16)
            return carry

        lax.fori_loop(0, length // part, one, 0)

    return pl.pallas_call(
        kernel,
        grid=(pairs,),
        in_specs=[
            pl.BlockSpec((length, LANES), spec_of(0)),
            pl.BlockSpec((length, LANES), spec_of(1)),
            pl.BlockSpec((length, LANES), spec_of(2)),
            whole(query_image.shape),
            whole(key_image.shape),
        ],
        out_specs=[
            pl.BlockSpec((length, LANES), lambda i: (0, i)),
            pl.BlockSpec((1, 2, length), lambda i: (i, 0, 0)),
        ],
        out_shape=[
            jax.ShapeDtypeStruct((length, width), bf16),
            jax.ShapeDtypeStruct((pairs, 2, length), f32),
        ],
        compiler_params=pltpu.CompilerParams(vmem_limit_bytes=vmem_bytes),
        cost_estimate=pl.CostEstimate(
            flops=16 * pairs * length * length * HD * 4,
            bytes_accessed=8 * length * width,
            transcendentals=2 * pairs * length * length,
        ),
        name="attend",
    )(queries, keys, values, query_image, key_image)


def attend_back(
    queries, keys, values, spec_of, width, attended, grads, log_total, query_image, key_image
):
    length = queries.shape[0]
    pairs = width // LANES
    part = min(256, length)
    score_scale = HD ** (-0.5)

    def kernel(
        q_ref, k_ref, v_ref, o_ref, g_ref, log_ref, qi_ref, ki_ref,
        dq_ref, dk_ref, dv_ref, key_sum, value_sum,
    ):
        key_block = k_ref[...]
        value_block = v_ref[...]
        key_turned = key_block.T
        key_parts = []
        value_parts = []
        for head in range(2):
            mine = head_lanes((length, LANES), 1, head)
            key_parts.append(jnp.where(mine, key_block, ki_ref[...]))
            value_parts.append(jnp.where(mine, value_block, jnp.zeros((), bf16)))
        key_sum[...] = jnp.zeros_like(key_sum)
        value_sum[...] = jnp.zeros_like(value_sum)
        sel_rows = lax.broadcasted_iota(jnp.int32, (8, LANES), 0)
        sel_lanes = lax.broadcasted_iota(jnp.int32, (8, LANES), 1)
        select = jnp.where(
            sel_rows == jnp.where(sel_lanes >= HD, 1, 0), jnp.ones((), f32), jnp.zeros((), f32)
        ).astype(bf16)

        def one(index, carry):
            rows = pl.ds(pl.multiple_of(index * part, part), part)
            query = q_ref[rows, :] * jnp.asarray(score_scale, bf16)
            grad = g_ref[rows, :]
            product = grad.astype(f32) * o_ref[rows, :].astype(f32)
            upper = product.astype(bf16)
            lower = (product - upper.astype(f32)).astype(bf16)
            inner = dot_nt(select, upper) + dot_nt(select, lower)
            turned = []
            for head in range(2):
                mine = head_lanes((part, LANES), 1, head)
                scores = dot_nt(key_parts[head], jnp.where(mine, query, qi_ref[rows, :]))
                chances = jnp.exp(scores - log_ref[0, pl.ds(head, 1), rows])
                grad_chances = dot_nt(value_parts[head], grad)
                grad_scores = (chances * (grad_chances - inner[head : head + 1, :])).astype(bf16)
                value_sum[head] += dot_nn(chances.astype(bf16), grad)
                key_sum[head] += dot_nn(grad_scores, query)
                result = dot_nn(key_turned, grad_scores)
                turned.append(result[head * HD : (head + 1) * HD, :])
            dq_ref[rows, :] = (jnp.concatenate(turned, axis=0).T * score_scale).astype(bf16)
            return carry

        lax.fori_loop(0, length // part, one, 0)
        lower_lanes = head_lanes((length, LANES), 1, 0)
        dk_ref[...] = jnp.where(lower_lanes, key_sum[0], key_sum[1]).astype(bf16)
        dv_ref[...] = jnp.where(lower_lanes, value_sum[0], value_sum[1]).astype(bf16)

    column = pl.BlockSpec((length, LANES), lambda i: (0, i))
    return pl.pallas_call(
        kernel,
        grid=(pairs,),
        in_specs=[
            pl.BlockSpec((length, LANES), spec_of(0)),
            pl.BlockSpec((length, LANES), spec_of(1)),
            pl.BlockSpec((length, LANES), spec_of(2)),
            column,
            column,
            pl.BlockSpec((1, 2, length), lambda i: (i, 0, 0)),
            whole(query_image.shape),
            whole(key_image.shape),
        ],
        out_specs=[column] * 3,
        out_shape=[jax.ShapeDtypeStruct((length, width), bf16)] * 3,
        scratch_shapes=[
            pltpu.VMEM((2, length, LANES), f32),
            pltpu.VMEM((2, length, LANES), f32),
        ],
        compiler_params=pltpu.CompilerParams(vmem_limit_bytes=vmem_bytes),
        cost_estimate=pl.CostEstimate(
            flops=40 * pairs * length * length * HD * 4,
            bytes_accessed=16 * length * width,
            transcendentals=2 * pairs * length * length,
        ),
        name="attend_back",
    )(queries, keys, values, attended, grads, log_total, query_image, key_image)


def gate_up_rows(normed, weight):
    tokens = normed.shape[0]
    tile = 256
    tiles = FF // tile
    chunk = 64

    def kernel(left_ref, gate_weight, up_weight, hidden_ref, gate_ref, up_ref, gate_sum, up_sum):
        gate_sum[...] = dot_nn(left_ref[...], gate_weight[...])
        up_sum[...] = dot_nn(left_ref[...], up_weight[...])

        def one(index, carry):
            rows = pl.ds(pl.multiple_of(index * chunk, chunk), chunk)
            gate = gate_sum[rows, :]
            up = up_sum[rows, :]
            hidden_ref[rows, :] = (gate / (1.0 + jnp.exp(-gate)) * up).astype(bf16)
            gate_ref[rows, :] = gate.astype(bf16)
            up_ref[rows, :] = up.astype(bf16)
            return carry

        lax.fori_loop(0, tokens // chunk, one, 0)

    out = pl.BlockSpec((tokens, tile), lambda i: (0, i))
    return pl.pallas_call(
        kernel,
        grid=(tiles,),
        in_specs=[
            whole(normed.shape),
            pl.BlockSpec((D, tile), lambda i: (0, i)),
            pl.BlockSpec((D, tile), lambda i: (0, i + tiles)),
        ],
        out_specs=[out] * 3,
        out_shape=[jax.ShapeDtypeStruct((tokens, FF), bf16)] * 3,
        scratch_shapes=[pltpu.VMEM((tokens, tile), f32), pltpu.VMEM((tokens, tile), f32)],
        compiler_params=pltpu.CompilerParams(vmem_limit_bytes=vmem_bytes),
        cost_estimate=pl.CostEstimate(
            flops=4 * tokens * D * FF, bytes_accessed=4 * D * FF + 6 * tokens * FF, transcendentals=0
        ),
        name="gate_up_rows",
    )(normed, weight, weight)


def gate_up_back(ffn_back, weight, gate, up):
    tokens = ffn_back.shape[0]
    tile = 256
    tiles = FF // tile
    chunk = 64

    def kernel(left_ref, weight_ref, gate_ref, up_ref, gate_back, up_back, total):
        total[...] = dot_nt(left_ref[...], weight_ref[...])

        def one(index, carry):
            rows = pl.ds(pl.multiple_of(index * chunk, chunk), chunk)
            grad = total[rows, :]
            gate_rows = gate_ref[rows, :].astype(f32)
            share = 1.0 / (1.0 + jnp.exp(-gate_rows))
            active = gate_rows * share
            up_back[rows, :] = (grad * active).astype(bf16)
            slope = share + active * (1.0 - share)
            gate_back[rows, :] = (grad * up_ref[rows, :].astype(f32) * slope).astype(bf16)
            return carry

        lax.fori_loop(0, tokens // chunk, one, 0)

    column = pl.BlockSpec((tokens, tile), lambda i: (0, i))
    return pl.pallas_call(
        kernel,
        grid=(tiles,),
        in_specs=[
            whole(ffn_back.shape),
            pl.BlockSpec((tile, D), lambda i: (i, 0)),
            column,
            column,
        ],
        out_specs=[column] * 2,
        out_shape=[jax.ShapeDtypeStruct((tokens, FF), bf16)] * 2,
        scratch_shapes=[pltpu.VMEM((tokens, tile), f32)],
        compiler_params=pltpu.CompilerParams(vmem_limit_bytes=vmem_bytes),
        cost_estimate=pl.CostEstimate(
            flops=2 * tokens * D * FF, bytes_accessed=2 * D * FF + 8 * tokens * FF, transcendentals=0
        ),
        name="gate_up_back",
    )(ffn_back, weight, gate, up)


def output_rows(attended, weight, embedded, image, post_table, pre_table):
    def body(value, rows, ins, consts, outs, scratch):
        hat = value * inverse_rms(value)
        image_rows = ins[1][rows, :1]
        mixed = ins[0][rows, :] + picked(image_rows, consts[0][...]) * hat
        outs[0][rows, :] = value
        outs[1][rows, :] = mixed
        outs[2][rows, :] = (
            mixed * inverse_rms(mixed) * picked(image_rows, consts[1][...])
        ).astype(bf16)

    return matmul_rows(
        "output_rows", [attended], weight, "nn", 256, [embedded, image], [post_table, pre_table],
        [(D, f32), (D, f32), (D, bf16)], [], body,
    )


def down_rows(hidden, weight, mixed, image, onehot, grad_patches, post_table, out_table, w_final):
    def before(ins, consts, outs, scratch):
        scratch[0][...] = dot_nt(ins[3][...], consts[2][...])

    def body(value, rows, ins, consts, outs, scratch):
        inverse = inverse_rms(value)
        hat = value * inverse
        image_rows = ins[1][rows, :1]
        post = picked(image_rows, consts[0][...])
        final_state = ins[0][rows, :] + post * hat
        centred = final_state - row_mean(final_state)
        spread = inverse_rms(centred)
        levelled = centred * spread
        scale = picked(image_rows, consts[1][...])
        outs[0][rows, :] = (levelled * scale).astype(bf16)
        grad = scratch[0][rows, :]
        scratch[1][rows, :] = grad * levelled
        back = grad * scale
        late = spread * (back - row_mean(back) - levelled * row_mean(back * levelled))
        outs[1][rows, :] = late
        scratch[2][rows, :] = late * hat
        back = late * post
        outs[2][rows, :] = (inverse * (back - hat * row_mean(back * hat))).astype(bf16)

    def after(ins, consts, outs, sums, scratch):
        outs[3][...] = dot_nn(outs[0][...], consts[2][...]).astype(bf16)
        one = ins[2][...]
        sums[0][...] += image_sums(one, scratch[1][...])
        sums[1][...] += image_sums(one, scratch[2][...])

    return matmul_rows(
        "down_rows", [hidden], weight, "nn", 256, [mixed, image, onehot, grad_patches],
        [post_table, out_table, w_final],
        [(D, bf16), (D, f32), (D, bf16), (PIN, bf16)], [8, 8], body,
        before=before, after=after, block_scratch=[(D, f32)] * 3,
    )


def ffn_back_rows(
    gate_back, up_back, weight, late, mixed, attn_out, image, onehot, post_table, pre_table
):
    def body(value, rows, ins, consts, outs, scratch):
        image_rows = ins[3][rows, :1]
        mixed_rows = ins[1][rows, :]
        inverse = inverse_rms(mixed_rows)
        hat = mixed_rows * inverse
        scratch[0][rows, :] = value * hat
        back = value * picked(image_rows, consts[1][...])
        early = ins[0][rows, :] + inverse * (back - hat * row_mean(back * hat))
        outs[0][rows, :] = early
        attn_rows = ins[2][rows, :]
        inverse = inverse_rms(attn_rows)
        hat = attn_rows * inverse
        scratch[1][rows, :] = early * hat
        back = early * picked(image_rows, consts[0][...])
        outs[1][rows, :] = (inverse * (back - hat * row_mean(back * hat))).astype(bf16)

    def after(ins, consts, outs, sums, scratch):
        one = ins[4][...]
        sums[0][...] += image_sums(one, scratch[0][...])
        sums[1][...] += image_sums(one, scratch[1][...])

    return matmul_rows(
        "ffn_back_rows", [gate_back, up_back], weight, "nt", 256,
        [late, mixed, attn_out, image, onehot], [post_table, pre_table],
        [(D, f32), (D, bf16)], [8, 8], body, after=after, block_scratch=[(D, f32)] * 2,
    )


def project_back_rows(
    project_back, weight, embedded, late, image, onehot, pre_table, w_embed
):
    def body(value, rows, ins, consts, outs, scratch):
        embedded_rows = ins[0][rows, :]
        inverse = inverse_rms(embedded_rows)
        hat = embedded_rows * inverse
        scratch[0][rows, :] = value * hat
        back = value * picked(ins[2][rows, :1], consts[0][...])
        early = inverse * (back - hat * row_mean(back * hat))
        outs[0][rows, :] = (early + ins[1][rows, :]).astype(bf16)

    def after(ins, consts, outs, sums, scratch):
        outs[1][...] = dot_nn(outs[0][...], consts[1][...]).astype(bf16)
        sums[0][...] += image_sums(ins[3][...], scratch[0][...])

    return matmul_rows(
        "project_back_rows", [project_back], weight, "nt", 256,
        [embedded, late, image, onehot], [pre_table, w_embed],
        [(D, bf16), (PIN, bf16)], [8], body, after=after, block_scratch=[(D, f32)],
    )


def turn_back(grad_q, grad_k, hats, inverses, cosine, sine, gains):
    tokens = grad_q.shape[0]
    block = min(256, tokens)
    chunk = 32

    def kernel(gq_ref, gk_ref, hat_ref, inv_ref, cos_ref, sin_ref, gain_ref, out_ref, sum_ref):
        @pl.when(pl.program_id(0) == 0)
        def _():
            sum_ref[...] = jnp.zeros_like(sum_ref)

        for which, grad_ref in enumerate((gq_ref, gk_ref)):
            gain = gain_ref[which : which + 1, :]

            def one(index, carry):
                rows = pl.ds(pl.multiple_of(index * chunk, chunk), chunk)
                first = first_lanes(chunk)
                cos_rows = cos_ref[rows, :]
                sin_rows = sin_ref[rows, :]
                pieces = []
                for lane in range(0, D, LANES):
                    part = grad_ref[rows, lane : lane + LANES].astype(f32)
                    pieces.append(part * cos_rows - swapped(part, first) * sin_rows)
                turned = jnp.concatenate(pieces, axis=1)
                hat = hat_ref[rows, which * D : (which + 1) * D].astype(f32)
                inverse = inv_ref[rows, which * LANES : which * LANES + 1]
                back = turned * gain
                out_ref[rows, which * D : (which + 1) * D] = (
                    inverse * (back - hat * row_mean(back * hat))
                ).astype(bf16)
                return carry + jnp.sum((turned * hat).reshape(chunk // 8, 8, D), axis=0)

            total = lax.fori_loop(0, block // chunk, one, jnp.zeros((8, D), f32))
            sum_ref[which : which + 1, :] += jnp.sum(total, axis=0, keepdims=True)

    row = lambda cols: pl.BlockSpec((block, cols), lambda i: (i, 0))
    return pl.pallas_call(
        kernel,
        grid=(tokens // block,),
        in_specs=[
            row(D), row(D), row(2 * D), row(2 * LANES), row(LANES), row(LANES), whole(gains.shape)
        ],
        out_specs=[row(2 * D), pl.BlockSpec((8, D), lambda i: (0, 0))],
        out_shape=[
            jax.ShapeDtypeStruct((tokens, 2 * D), bf16),
            jax.ShapeDtypeStruct((8, D), f32),
        ],
        compiler_params=pltpu.CompilerParams(vmem_limit_bytes=vmem_bytes),
        cost_estimate=pl.CostEstimate(
            flops=40 * tokens * D, bytes_accessed=12 * tokens * D, transcendentals=0
        ),
        name="turn_back",
    )(grad_q, grad_k, hats, inverses, cosine, sine, gains)


def to_strips(tiles):
    micros = tiles.shape[0]
    count = lax.axis_size("rows")
    parts = count // micros
    me = lax.axis_index("rows")
    slots = []
    for shift in range(micros):
        pairs = [(q, ((q % micros - shift) % micros) * parts + q // micros) for q in range(count)]
        sent = lax.dynamic_index_in_dim(tiles, (me % micros - shift) % micros, 0, keepdims=False)
        if any(a != b for a, b in pairs):
            sent = lax.ppermute(sent, "rows", pairs)
        slots.append(sent)
    stacked = jnp.stack(slots)
    order = (jnp.arange(micros) - me // parts) % micros
    ordered = jnp.concatenate(
        [lax.dynamic_index_in_dim(stacked, order[d], 0) for d in range(micros)], axis=0
    )
    kinds, height, width = ordered.shape[1:]
    return ordered.transpose(1, 0, 2, 3).reshape(kinds, micros * height, width)


def from_strips(strip, micros):
    count = lax.axis_size("rows")
    parts = count // micros
    me = lax.axis_index("rows")
    kinds, height, width = strip.shape
    tiles = strip.reshape(kinds, micros, height // micros, width).transpose(1, 0, 2, 3)
    slots = []
    for shift in range(micros):
        pairs = [(((q % micros - shift) % micros) * parts + q // micros, q) for q in range(count)]
        sent = lax.dynamic_index_in_dim(tiles, (me // parts + shift) % micros, 0, keepdims=False)
        if any(a != b for a, b in pairs):
            sent = lax.ppermute(sent, "rows", pairs)
        slots.append(sent)
    stacked = jnp.stack(slots)
    return jnp.concatenate(
        [
            lax.dynamic_index_in_dim(stacked, (me % micros - m) % micros, 0)
            for m in range(micros)
        ],
        axis=0,
    )


def neighbour_pairs(axis, parts):
    count = lax.axis_size(axis)
    ups = [(i, i + 1) for i in range(count - 1) if (i + 1) % parts != 0]
    return ups, [(b, a) for a, b in ups]


def neighbours(values, axis, dim, parts):
    ups, downs = neighbour_pairs(axis, parts)
    head = lax.slice_in_dim(values, 0, 1, axis=dim)
    tail = lax.slice_in_dim(values, values.shape[dim] - 1, values.shape[dim], axis=dim)
    if len(ups) == 0:
        return jnp.zeros_like(head), jnp.zeros_like(tail)
    return lax.ppermute(tail, axis, ups), lax.ppermute(head, axis, downs)


def sides(parts):
    return (("cols", 1, lax.axis_size("cols")), ("rows", 0, parts))


def extract_patches(strip, parts):
    for axis, dim, span in sides(parts):
        before, after = neighbours(strip, axis, dim + 1, span)
        strip = jnp.concatenate([before, strip, after], axis=dim + 1)
    kinds, height, width = strip.shape
    sets = kinds // CHANNELS
    rows, cols = height // 2 - 1, width // 2 - 1
    cells = (
        strip.reshape(sets, CHANNELS, rows + 1, 2, cols + 1, 2)
        .transpose(0, 2, 4, 1, 3, 5)
        .reshape(sets, rows + 1, cols + 1, CELL)
    )
    windows = [cells[:, u : u + rows, v : v + cols] for u in range(2) for v in range(2)]
    return jnp.concatenate(windows, axis=-1).reshape(sets, rows * cols, PIN)


def fold_patches(pieces, rows, cols, parts):
    grid = pieces.astype(f32).reshape(rows, cols, 2, 2, CELL)
    cells = jnp.zeros((rows + 1, cols + 1, CELL), f32)
    for u in range(2):
        for v in range(2):
            cells = cells + jnp.pad(grid[:, :, u, v], ((u, 1 - u), (v, 1 - v), (0, 0)))
    for axis, dim, span in sides(parts):
        before, after = neighbours(cells, axis, dim, span)
        middle = list(cells.shape)
        middle[dim] -= 2
        cells = cells + jnp.concatenate([before, jnp.zeros(middle, f32), after], axis=dim)
    canvas = (
        cells.reshape(rows + 1, cols + 1, CHANNELS, 2, 2)
        .transpose(2, 0, 3, 1, 4)
        .reshape(CHANNELS, 2 * rows + 2, 2 * cols + 2)
    )
    return canvas[:, 1:-1, 1:-1]


def window_order(weight):
    rows = weight.shape[0]
    return weight.reshape(rows, CHANNELS, 2, 2, 2, 2).transpose(0, 2, 4, 1, 3, 5).reshape(rows, PIN)


def channel_order(weight):
    rows = weight.shape[0]
    return weight.reshape(rows, 2, 2, CHANNELS, 2, 2).transpose(0, 3, 1, 4, 2, 5).reshape(rows, PIN)


def strip_layout(heights, seq_rows):
    starts = jnp.cumsum(heights) - heights
    rows_all = jnp.arange(seq_rows, dtype=jnp.int32)
    image_of = jnp.sum((rows_all[:, None] >= starts[None, 1:]).astype(jnp.int32), axis=1)
    start_of = jnp.sum(
        jnp.where(
            image_of[:, None] == jnp.arange(IMGS, dtype=jnp.int32)[None, :], starts[None, :], 0
        ),
        axis=1,
    )
    return (image_of, rows_all - start_of)


def rope_tables(row_place, column):
    quarter = HD // 4
    frequency = 10000.0 ** (-jnp.arange(quarter, dtype=f32) / quarter)
    row_angle = row_place.astype(f32)[:, None] * frequency[None, :]
    col_angle = column.astype(f32)[:, None] * frequency[None, :]
    angles = jnp.concatenate([row_angle, row_angle, col_angle, col_angle] * 2, axis=1)
    sign = jnp.where(jnp.arange(LANES) % 32 < 16, -1.0, 1.0)
    return (jnp.cos(angles), jnp.sin(angles) * sign[None, :])


def gather_all(shard):
    return lax.all_gather(shard, ALL, axis=0, tiled=True)


def scatter_all(part):
    return lax.psum_scatter(part, ALL, scatter_dimension=0, tiled=True)


def bits_of(axis):
    return lax.axis_size(axis).bit_length() - 1


def orders():
    first = [("fsdp", bit) for bit in range(bits_of("fsdp"))]
    main = [("cols", 0), ("rows", 0), ("cols", 1)]
    rest = [("rows", bit) for bit in range(1, bits_of("rows"))]
    rest += [("cols", bit) for bit in range(2, bits_of("cols"))]
    return [first + main[turn:] + main[:turn] + rest for turn in range(3)]


def block_masks(order):
    base = {"fsdp": 0, "cols": bits_of("fsdp"), "rows": bits_of("fsdp") + bits_of("cols")}
    steps = len(order)
    return [
        sum(
            ((index >> (steps - 1 - step)) & 1) << (base[axis] + bit)
            for step, (axis, bit) in enumerate(order)
        )
        for index in range(1 << steps)
    ]


def swap(values, axis, bit):
    return lax.ppermute(values, axis, [(i, i ^ (1 << bit)) for i in range(lax.axis_size(axis))])


def gather_near(shards_, picks):
    steps = [list(reversed(order)) for order in picks]
    held = list(shards_)
    for step in range(len(steps[0])):
        received = [swap(value, *steps[k][step]) for k, value in enumerate(held)]
        if step == len(steps[0]) - 1:
            return list(zip(held, received))
        held = [jnp.concatenate(pair, axis=0) for pair in zip(held, received)]


def scatter_near(parts, picks):
    terms = [[part] for part in parts]
    kind = [part.dtype for part in parts]
    half = [part.shape[0] // 2 for part in parts]
    total = lambda values: sum(value.astype(f32) for value in values)
    for step in range(len(picks[0])):
        sent = []
        for k in range(len(parts)):
            sent.append(total([term[half[k] :] for term in terms[k]]).astype(kind[k]))
        received = [swap(value, *picks[k][step]) for k, value in enumerate(sent)]
        for k in range(len(parts)):
            terms[k] = [term[: half[k]] for term in terms[k]] + [received[k]]
            half[k] //= 2
    return [total(values) for values in terms]


def exchange_heads(parts, micros):
    groups = [[m * parts + s for s in range(parts)] for m in range(micros)]

    def spread(values):
        return lax.all_to_all(
            values, "rows", split_axis=1, concat_axis=0, tiled=True, axis_index_groups=groups
        )

    def collect(values):
        return lax.all_to_all(
            values, "rows", split_axis=0, concat_axis=1, tiled=True, axis_index_groups=groups
        )

    return spread, collect


def shards(
    latent,
    time_embed,
    image_rows,
    pred_grad,
    embed_weight,
    adaptive_weight,
    project_weight,
    output_weight,
    gate_up_weight,
    down_weight,
    final_weight,
    norm_gains,
):
    micros = latent.shape[0]
    row_devices = lax.axis_size("rows")
    parts = row_devices // micros
    row_index = lax.axis_index("rows")
    micro, piece = row_index // parts, row_index % parts
    device = (row_index * lax.axis_size("cols") + lax.axis_index("cols")) * lax.axis_size(
        "fsdp"
    ) + lax.axis_index("fsdp")
    rows = latent.shape[3] // 2 * micros
    cols = latent.shape[4] // 2
    tokens = rows * cols
    seq_rows = rows * parts
    length = seq_rows * cols

    devices = lax.axis_size(ALL)
    share = D // devices
    near = share % 16 == 0
    picks = orders()
    place = None
    if near:
        place = (device.astype(jnp.int32).reshape(1), [block_masks(order) for order in picks])

    small = jnp.concatenate(
        [
            window_order(embed_weight),
            window_order(final_weight),
            norm_gains,
            jnp.zeros((norm_gains.shape[0], 2 * LANES - 2 * PIN - 6), bf16),
        ],
        axis=1,
    )
    temb = lax.dynamic_index_in_dim(time_embed, micro, 0, keepdims=False)[0, 0]
    condition = jax.nn.silu(temb).astype(bf16)
    if near:
        wide = condition.reshape(-1, 2 * LANES)
        both = gather_near([jnp.concatenate([small, wide], axis=0)], picks[:1])[0]
        both = jnp.concatenate(both, axis=0).reshape(devices, share + wide.shape[0], 2 * LANES)
        small = both[:, :share]
        conditions = both[:, share:].reshape(devices * IMGS, condition.shape[1])
        source = jnp.asarray(place[1][0], jnp.int32)
        chosen = ((jnp.arange(devices, dtype=jnp.int32) ^ device)[:, None] == source[None, :]).astype(bf16)
        small = dot_nn(chosen, small.reshape(devices, share * 2 * LANES)).astype(bf16)
        small = small.reshape(D, 2 * LANES)
    else:
        small = gather_all(small)
        conditions = gather_all(condition)
    w_embed = small[:, :PIN]
    w_final = small[:, PIN : 2 * PIN]
    gains = small[:, 2 * PIN : 2 * PIN + 6].astype(f32).T

    rows_held = adaptive_weight.shape[0]
    conditions = lax.dynamic_slice_in_dim(conditions, device * rows_held, rows_held, axis=1)
    per_image = dot_nn(conditions, adaptive_weight)
    if near:
        per_image = scatter_near([per_image], picks[:1])[0]
        thirds = [project_weight[:, k * D : (k + 1) * D] for k in range(3)]
        project_pieces = [piece for pair in gather_near(thirds, picks) for piece in pair]
    else:
        per_image = scatter_all(per_image)
        project_pieces = [gather_all(project_weight)]
    w_output = gather_all(output_weight)
    w_gate_up = gather_all(gate_up_weight)
    w_down = gather_all(down_weight)

    tiles = jnp.concatenate([latent[:, 0], pred_grad[:, 0]], axis=1)
    patches, grad_patches = extract_patches(to_strips(tiles), parts)

    heights = lax.dynamic_index_in_dim(image_rows, micro, 0, keepdims=False)[0, 0]
    row_image, row_place = strip_layout(heights, seq_rows)
    first_row = piece * rows
    my_image = lax.dynamic_slice_in_dim(row_image, first_row, rows)
    my_place = lax.dynamic_slice_in_dim(row_place, first_row, rows)
    token_image = jnp.repeat(my_image, cols)
    cosine, sine = rope_tables(
        jnp.repeat(my_place, cols), jnp.tile(jnp.arange(cols, dtype=jnp.int32), rows)
    )
    image = jnp.broadcast_to(token_image[:, None], (tokens, LANES))
    onehot = (token_image[None, :] == jnp.arange(8, dtype=jnp.int32)[:, None]).astype(bf16)
    strip_image = jnp.repeat(row_image, cols)
    head_lane = jnp.arange(LANES, dtype=jnp.int32)[None, :] % HD
    same = strip_image[:, None] == head_lane
    query_image = jnp.where(same, -mask_level, 0.0).astype(bf16)
    key_image = jnp.where(same | (head_lane >= IMGS), 0.0, mask_level).astype(bf16)

    modulation = per_image.reshape(IMGS, 5, D)
    scale_attn = 1.0 + modulation[:, 0]
    gate_attn = jnp.tanh(modulation[:, 1])
    scale_ffn = 1.0 + modulation[:, 2]
    gate_ffn = jnp.tanh(modulation[:, 3])
    scale_out = 1.0 + modulation[:, 4]
    table = lambda values: jnp.concatenate([values, values], axis=0)
    attn_pre = table(scale_attn * gains[0])
    attn_post = table(gate_attn * gains[3])
    ffn_pre = table(scale_ffn * gains[4])
    ffn_post = table(gate_ffn * gains[5])
    out_scale = table(scale_out)
    turn_gains = jnp.concatenate([gains[1:3], jnp.zeros((6, D), f32)], axis=0)

    embedded, normed, projected, hats, inverses, w_project = project_rows(
        patches, image, cosine, sine, w_embed, attn_pre, project_pieces, turn_gains, place
    )
    if parts == 1:
        pairs = D // LANES
        heads = (projected, projected, projected)
        spec_of = lambda which: (lambda i: (0, which * pairs + i))
        width = D
    else:
        spread, collect = exchange_heads(parts, micros)
        heads = tuple(spread(projected[:, w * D : (w + 1) * D]) for w in range(3))
        spec_of = lambda which: (lambda i: (0, i))
        width = D // parts
    attended_heads, log_total = attend(*heads, spec_of, width, query_image, key_image)
    attended = attended_heads if parts == 1 else collect(attended_heads)
    attn_out, mixed, normed_ffn = output_rows(
        attended, w_output, embedded, image, attn_post, ffn_pre
    )
    hidden, gate, up = gate_up_rows(normed_ffn, w_gate_up)
    final, late, ffn_back, pieces, sum_out, sum_ffn_post = down_rows(
        hidden, w_down, mixed, image, onehot, grad_patches, ffn_post, out_scale, w_final
    )
    down_grad = dot_tn(hidden, ffn_back).astype(bf16)
    ffn_back, down_grad = lax.optimization_barrier((ffn_back, down_grad))
    down_share = scatter_all(down_grad)
    prediction = from_strips(fold_patches(pieces, rows, cols, parts), micros)

    gate_back, up_back = gate_up_back(ffn_back, w_down, gate, up)
    gate_grad = dot_tn(normed_ffn, gate_back).astype(bf16)
    gate_back, gate_grad = lax.optimization_barrier((gate_back, gate_grad))
    gate_share = scatter_all(gate_grad)
    up_grad = dot_tn(normed_ffn, up_back).astype(bf16)
    up_back, up_grad = lax.optimization_barrier((up_back, up_grad))
    up_share = scatter_all(up_grad)
    early, attn_back, sum_ffn_pre, sum_attn_post = ffn_back_rows(
        gate_back, up_back, w_gate_up, late, mixed, attn_out, image, onehot, attn_post, ffn_pre
    )
    grad_attended = dot_nt(attn_back, w_output).astype(bf16)
    if parts > 1:
        grad_attended = spread(grad_attended)
    grads = attend_back(
        *heads, spec_of, width, attended_heads, grad_attended, log_total, query_image, key_image
    )
    if parts > 1:
        grads = tuple(collect(grad) for grad in grads)
    turned, sum_turn = turn_back(grads[0], grads[1], hats, inverses, cosine, sine, turn_gains)
    project_back = jnp.concatenate([turned, grads[2]], axis=1)
    if near:
        parts_held = [
            attention_grads(k, normed, project_back, attended, attn_back, place) for k in range(3)
        ]
        held = scatter_near(parts_held, picks)
        project_share = jnp.concatenate([value[:, :D] for value in held], axis=1)
        output_share = jnp.concatenate([value[:, D:] for value in held], axis=1)
    else:
        project_share = scatter_all(dot_tn(normed, project_back).astype(bf16))
        output_share = scatter_all(dot_tn(attended, attn_back).astype(bf16))
    embed_back, grad_pieces, sum_attn_pre = project_back_rows(
        project_back, w_project, embedded, early, image, onehot, attn_pre, w_embed
    )
    latent_grad = from_strips(fold_patches(grad_pieces, rows, cols, parts), micros)

    sum_attn_pre, sum_attn_post = sum_attn_pre[:IMGS], sum_attn_post[:IMGS]
    sum_ffn_pre, sum_ffn_post = sum_ffn_pre[:IMGS], sum_ffn_post[:IMGS]
    grad_modulation = jnp.stack(
        [
            gains[0] * sum_attn_pre,
            (1.0 - gate_attn * gate_attn) * gains[3] * sum_attn_post,
            gains[4] * sum_ffn_pre,
            (1.0 - gate_ffn * gate_ffn) * gains[5] * sum_ffn_post,
            sum_out[:IMGS],
        ],
        axis=1,
    ).reshape(IMGS, 5 * D)
    if near:
        wide = grad_modulation.astype(bf16).reshape(16, -1)
        pair = gather_near([wide], picks[:1])[0]
        grad_modulations = jnp.concatenate(pair, axis=0).astype(f32).reshape(-1, 5 * D)
    else:
        grad_modulations = gather_all(grad_modulation)
    adaptive_share = lax.dot_general(
        conditions.astype(f32),
        grad_modulations,
        (((0,), (0,)), ((), ())),
        precision=highest,
        preferred_element_type=f32,
    )
    gain_grads = jnp.stack(
        [
            jnp.sum(scale_attn * sum_attn_pre, axis=0),
            sum_turn[0],
            sum_turn[1],
            jnp.sum(gate_attn * sum_attn_post, axis=0),
            jnp.sum(scale_ffn * sum_ffn_pre, axis=0),
            jnp.sum(gate_ffn * sum_ffn_post, axis=0),
        ],
        axis=1,
    )
    small_grads = jnp.concatenate(
        [
            dot_tn(embed_back, patches),
            dot_tn(final, grad_patches),
            gain_grads,
            jnp.zeros((D, 2 * LANES - 2 * PIN - 6), f32),
        ],
        axis=1,
    )
    if near:
        chosen = ((source ^ device)[:, None] == jnp.arange(devices, dtype=jnp.int32)[None, :]).astype(f32)
        small_grads = jnp.dot(
            chosen, small_grads.reshape(devices, share * 2 * LANES), precision=highest
        ).reshape(D, 2 * LANES)
        small_share = scatter_near([small_grads], picks[:1])[0]
    else:
        small_share = scatter_all(small_grads)
    return (
        prediction[:, None],
        latent_grad[:, None],
        channel_order(small_share[:, :PIN]),
        adaptive_share,
        project_share.astype(f32),
        output_share.astype(f32),
        jnp.concatenate([gate_share, up_share], axis=1).astype(f32),
        down_share.astype(f32),
        channel_order(small_share[:, PIN : 2 * PIN]),
        small_share[:, 2 * PIN : 2 * PIN + 6],
    )


def solution(mesh):
    canvas = P(None, "fsdp", None, "rows", "cols")
    weight = P(ALL, None)
    return jax.shard_map(
        shards,
        mesh=mesh,
        in_specs=(canvas, P(None, "fsdp", "cols", None, None), P(None, "fsdp", "cols", None), canvas)
        + (weight,) * 8,
        out_specs=(canvas, canvas) + (weight,) * 8,
        check_vma=False,
    )
```

```python
from functools import partial

import jax
import jax.numpy as jnp
from jax import lax
from jax.experimental import pallas as pl
from jax.experimental.pallas import tpu as pltpu
from jax.sharding import PartitionSpec as P

D = 1536
HEADS = 24
HD = 64
FF = 4096
CHANNELS = 4
PIN = 64
IMGS = 4
CELL = 16
LANES = 128
ALL = ("rows", "cols", "fsdp")

epsilon = 1e-06
highest = lax.Precision.HIGHEST
mask_level = 256.0
f32 = jnp.float32
bf16 = jnp.bfloat16
vmem_bytes = 60 * 1024 * 1024
SHRINK = 2
WAIT_FOR_GATE_UP = False


def estimate(flops, bytes_accessed, transcendentals):
    return pl.CostEstimate(
        flops=flops // SHRINK, bytes_accessed=bytes_accessed // SHRINK, transcendentals=0
    )


def ordered(kernel, count):
    return lambda *refs: kernel(*refs[count:])


def unread(arrays):
    return [pl.BlockSpec(memory_space=pl.ANY)] * len(arrays)


def held_until(value, *others):
    return pl.pallas_call(
        lambda *refs: None,
        in_specs=unread((value,) + others),
        out_specs=pl.BlockSpec(memory_space=pl.ANY),
        out_shape=jax.ShapeDtypeStruct(value.shape, value.dtype),
        input_output_aliases={0: 0},
        name="held_until",
    )(value, *others)


def dot_nn(left, right):
    return lax.dot_general(left, right, (((1,), (0,)), ((), ())), preferred_element_type=f32)


def dot_nt(left, right):
    return lax.dot_general(left, right, (((1,), (1,)), ((), ())), preferred_element_type=f32)


def dot_tn(left, right):
    return lax.dot_general(left, right, (((0,), (0,)), ((), ())), preferred_element_type=f32)


def row_mean(values):
    return jnp.mean(values, axis=-1, keepdims=True)


def inverse_rms(values):
    return lax.rsqrt(row_mean(values * values) + epsilon)


def whole(shape):
    zeros = (0,) * len(shape)
    return pl.BlockSpec(shape, lambda i: zeros, pipeline_mode=pl.Buffered(1))


def picked(image, table):
    choice = table[IMGS - 1 : IMGS, :]
    for index in range(IMGS - 2, -1, -1):
        choice = jnp.where(image == index, table[index : index + 1, :], choice)
    return choice


def image_sums(onehot, product):
    upper = product.astype(bf16)
    lower = (product - upper.astype(f32)).astype(bf16)
    return dot_nn(onehot, upper) + dot_nn(onehot, lower)


def matmul_rows(
    name, lefts, weight, kind, depth_tile, row_ins, consts, row_outs, sum_rows, chunk_body,
    before=None, after=None, block_scratch=(), wait=(), shape=None, column=0,
):
    tokens = lefts[0].shape[0]
    depth, width = shape or (weight.shape if kind == "nn" else weight.shape[::-1])
    block = min(256, tokens)
    chunk = 64
    tiles = depth // depth_tile
    blocks = tokens // block
    counts = (len(lefts), len(row_ins), len(consts), len(row_outs), len(sum_rows))
    ends = []
    for left in lefts:
        ends.append((ends[-1] if ends else 0) + left.shape[1] // depth_tile)
    starts = [0] + ends[:-1]

    def kernel(*refs):
        refs = list(refs)
        take = lambda n: [refs.pop(0) for _ in range(n)]
        left_refs = take(counts[0])
        weight_ref = take(1)[0]
        in_refs, const_refs = take(counts[1]), take(counts[2])
        out_refs, sum_refs = take(counts[3]), take(counts[4])
        total = refs.pop(0)
        scratch = refs
        step = pl.program_id(0)
        product = dot_nn if kind == "nn" else dot_nt

        @pl.when(step == 0)
        def _():
            total[...] = product(left_refs[0][...], weight_ref[...])
            for ref in sum_refs:
                ref[...] = jnp.zeros_like(ref)

        for left_ref, low, high in zip(left_refs, starts, ends):

            @pl.when((step >= max(low, 1)) & (step < high))
            def _():
                total[...] += product(left_ref[...], weight_ref[...])

        @pl.when(step >= tiles)
        def _():
            start = pl.multiple_of((step - tiles) * block, block)
            if before is not None:
                before(in_refs, const_refs, out_refs, scratch)
            for low in range(0, block, chunk):
                chunk_body(
                    total[pl.ds(pl.multiple_of(start + low, chunk), chunk), :],
                    pl.ds(low, chunk), in_refs, const_refs, out_refs, scratch,
                )
            if after is not None:
                after(in_refs, const_refs, out_refs, sum_refs, scratch)

    def row_map(i):
        return (jnp.maximum(i - tiles, 0), 0)

    def col_map(i):
        return (0, jnp.maximum(i - tiles, 0))

    def left_map(low, high):
        return lambda i: (0, jnp.clip(i - low, 0, high - low - 1))

    if kind == "nn":
        weight_spec = pl.BlockSpec(
            (depth_tile, width), lambda i: (jnp.minimum(i, tiles - 1), column)
        )
    else:
        weight_spec = pl.BlockSpec((width, depth_tile), lambda i: (0, jnp.minimum(i, tiles - 1)))
    in_specs = [
        pl.BlockSpec((tokens, depth_tile), left_map(low, high)) for low, high in zip(starts, ends)
    ]
    in_specs.append(weight_spec)
    for array in row_ins:
        if array.shape[0] == tokens:
            in_specs.append(pl.BlockSpec((block, array.shape[1]), row_map))
        else:
            in_specs.append(pl.BlockSpec((array.shape[0], block), col_map))
    in_specs += [whole(array.shape) for array in consts]
    out_specs = [pl.BlockSpec((block, cols), row_map) for cols, _ in row_outs]
    out_specs += [pl.BlockSpec((count, width), lambda i: (0, 0)) for count in sum_rows]
    out_shape = [jax.ShapeDtypeStruct((tokens, cols), kind_) for cols, kind_ in row_outs]
    out_shape += [jax.ShapeDtypeStruct((count, width), f32) for count in sum_rows]
    return pl.pallas_call(
        ordered(kernel, len(wait)),
        grid=(tiles + blocks,),
        in_specs=unread(wait) + in_specs,
        out_specs=out_specs,
        out_shape=out_shape,
        scratch_shapes=[pltpu.VMEM((tokens, width), f32)]
        + [pltpu.VMEM((block, cols), kind_) for cols, kind_ in block_scratch],
        compiler_params=pltpu.CompilerParams(vmem_limit_bytes=vmem_bytes),
        cost_estimate=estimate(
            flops=2 * tokens * width * depth,
            bytes_accessed=2 * (width * depth + tokens * depth) + 8 * tokens * width,
            transcendentals=0,
        ),
        name=name,
    )(*wait, *lefts, weight, *row_ins, *consts)


def swapped(values, first):
    return jnp.where(first, pltpu.roll(values, LANES - 16, 1), pltpu.roll(values, 16, 1))


def first_lanes(rows):
    lane = lax.broadcasted_iota(jnp.int32, (rows, LANES), 1)
    return lax.rem(lane, 32) < 16


def project_rows(patches, image, cosine, sine, w_embed, pre_table, w_project, gains):
    tokens = patches.shape[0]
    chunk = min(128, tokens)
    tile = 256
    blocks = D // tile

    def kernel(
        patches_ref, image_ref, cos_ref, sin_ref, embed_ref, pre_ref, weight_ref, gain_ref,
        embedded_ref, normed_ref, out_ref, hat_ref, inverse_ref, total,
    ):
        step = pl.program_id(0)

        @pl.when(step == 0)
        def _():
            total[...] = dot_nt(patches_ref[...], embed_ref[...])

            for low in range(0, tokens, chunk):
                rows = pl.ds(low, chunk)
                value = total[rows, :]
                embedded_ref[rows, :] = value
                normed_ref[rows, :] = (
                    value * inverse_rms(value) * picked(image_ref[rows, :1], pre_ref[...])
                ).astype(bf16)

        for index in range(blocks):
            cols = slice(index * tile, (index + 1) * tile)
            total[:, cols] = dot_nn(normed_ref[...], weight_ref[:, cols])

        @pl.when(step < 2)
        def _():
            gain = gain_ref[pl.ds(step, 1), :]

            for low in range(0, tokens, chunk):
                rows = pl.ds(low, chunk)
                value = total[rows, :]
                inverse = inverse_rms(value)
                hat = value * inverse
                hat_ref[rows, :] = hat.astype(bf16)
                inverse_ref[rows, :] = jnp.broadcast_to(inverse, (chunk, LANES))
                scaled = hat * gain
                first = first_lanes(chunk)
                cos_rows = cos_ref[rows, :]
                sin_rows = sin_ref[rows, :]
                for lane in range(0, D, LANES):
                    part = scaled[:, lane : lane + LANES]
                    turned = part * cos_rows + swapped(part, first) * sin_rows
                    out_ref[rows, lane : lane + LANES] = turned.astype(bf16)

        @pl.when(step == 2)
        def _():
            out_ref[...] = total[...].astype(bf16)

    return pl.pallas_call(
        kernel,
        grid=(3,),
        in_specs=[
            whole(patches.shape),
            whole(image.shape),
            whole(cosine.shape),
            whole(sine.shape),
            whole(w_embed.shape),
            whole(pre_table.shape),
            pl.BlockSpec((D, D), lambda i: (0, i)),
            whole(gains.shape),
        ],
        out_specs=[
            pl.BlockSpec((tokens, D), lambda i: (0, 0), pipeline_mode=pl.Buffered(1)),
            pl.BlockSpec((tokens, D), lambda i: (0, 0), pipeline_mode=pl.Buffered(1)),
            pl.BlockSpec((tokens, D), lambda i: (0, i)),
            pl.BlockSpec((tokens, D), lambda i: (0, jnp.minimum(i, 1))),
            pl.BlockSpec((tokens, LANES), lambda i: (0, jnp.minimum(i, 1))),
        ],
        out_shape=[
            jax.ShapeDtypeStruct((tokens, D), f32),
            jax.ShapeDtypeStruct((tokens, D), bf16),
            jax.ShapeDtypeStruct((tokens, 3 * D), bf16),
            jax.ShapeDtypeStruct((tokens, 2 * D), bf16),
            jax.ShapeDtypeStruct((tokens, 2 * LANES), f32),
        ],
        scratch_shapes=[pltpu.VMEM((tokens, D), f32)],
        compiler_params=pltpu.CompilerParams(vmem_limit_bytes=vmem_bytes),
        cost_estimate=estimate(
            flops=6 * tokens * D * D, bytes_accessed=6 * D * D + 24 * tokens * D, transcendentals=0
        ),
        name="project_rows",
    )(patches, image, cosine, sine, w_embed, pre_table, w_project, gains)


def arrange(pairs, place, used=None):
    count = len(pairs)
    devices = len(place[1][0])
    half = devices // 2
    stride = pairs[0][0].shape[0] // half
    share = stride if used is None else used
    width = pairs[0][0].shape[1]

    def kernel(*refs):
        me_ref, out_ref, sems = refs[2 * count :]
        step = pl.program_id(0)
        for part in range(count):

            @pl.when(step == part)
            def _():
                listed = []
                for index, mask in enumerate(place[1][part]):
                    low = pl.multiple_of((me_ref[0] ^ mask) * share, share)
                    listed.append(
                        pltpu.make_async_copy(
                            refs[2 * part + index // half].at[
                                pl.ds(index % half * stride, share), :
                            ],
                            out_ref.at[pl.ds(low, share), :],
                            sems.at[index],
                        )
                    )
                for copy in listed:
                    copy.start()
                for copy in listed:
                    copy.wait()

    return pl.pallas_call(
        kernel,
        grid=(count,),
        in_specs=[pl.BlockSpec(memory_space=pl.ANY)] * (2 * count)
        + [pl.BlockSpec(memory_space=pltpu.SMEM)],
        out_specs=pl.BlockSpec((devices * share, width), lambda i: (0, i)),
        out_shape=jax.ShapeDtypeStruct((devices * share, count * width), bf16),
        scratch_shapes=[pltpu.SemaphoreType.DMA((devices,))],
        compiler_params=pltpu.CompilerParams(vmem_limit_bytes=vmem_bytes),
        cost_estimate=estimate(
            flops=0, bytes_accessed=4 * devices * share * count * width, transcendentals=0
        ),
        name="arrange",
    )(*[value for pair in pairs for value in pair], place[0])


def small_grads_near(embed_back, patches, final, grad_patches, rows, place):
    masks = place[1][0]
    share = D // len(masks)
    half = len(masks) // 2

    def kernel(e_ref, p_ref, f_ref, g_ref, rows_ref, me_ref, kept_ref, sent_ref, held, sems):
        held[:, :PIN] = dot_tn(e_ref[...], p_ref[...])
        held[:, PIN : 2 * PIN] = dot_tn(f_ref[...], g_ref[...])
        tall = jnp.concatenate([rows_ref[...], jnp.zeros((LANES - 8, D), f32)], axis=0)
        held[:, LANES:] = tall.T
        listed = []
        for index, mask in enumerate(masks):
            low = pl.multiple_of((me_ref[0] ^ mask) * share, share)
            target = kept_ref if index < half else sent_ref
            listed.append(
                pltpu.make_async_copy(
                    held.at[pl.ds(low, share), :],
                    target.at[pl.ds(index % half * share, share), :],
                    sems.at[index],
                )
            )
        for copy in listed:
            copy.start()
        for copy in listed:
            copy.wait()

    return pl.pallas_call(
        kernel,
        in_specs=[pl.BlockSpec(memory_space=pltpu.VMEM)] * 5
        + [pl.BlockSpec(memory_space=pltpu.SMEM)],
        out_specs=[pl.BlockSpec(memory_space=pl.ANY)] * 2,
        out_shape=[jax.ShapeDtypeStruct((D // 2, 2 * LANES), f32)] * 2,
        scratch_shapes=[
            pltpu.VMEM((D, 2 * LANES), f32),
            pltpu.SemaphoreType.DMA((len(masks),)),
        ],
        compiler_params=pltpu.CompilerParams(vmem_limit_bytes=vmem_bytes),
        cost_estimate=estimate(
            flops=4 * patches.shape[0] * D * PIN, bytes_accessed=8 * patches.shape[0] * D,
            transcendentals=0,
        ),
        name="small_grads_near",
    )(embed_back, patches, final, grad_patches, rows, place[0])


def gain_rows(sums, factors, scales, turn_sums):
    wide = 5 * D // 2

    def kernel(*refs):
        sum_refs, factor_refs = refs[:5], refs[5:10]
        scale_refs, turn_ref, rows_ref, out_ref = refs[10:14], refs[14], refs[15], refs[16]
        rows_ref[...] = jnp.zeros_like(rows_ref)
        for spot, index in enumerate((0, 3, 4, 5)):
            rows_ref[index : index + 1, :] = jnp.sum(
                scale_refs[spot][...] * sum_refs[spot][:IMGS, :], axis=0, keepdims=True
            )
        rows_ref[1:3, :] = turn_ref[0:2, :]
        flat = [factor_refs[k][...] * sum_refs[k][:IMGS, :] for k in range(5)]
        middle = wide - 2 * D
        out_ref[:IMGS, :] = jnp.concatenate(flat[:2] + [flat[2][:, :middle]], axis=1).astype(bf16)
        out_ref[IMGS:, :] = jnp.concatenate([flat[2][:, middle:]] + flat[3:], axis=1).astype(bf16)

    return pl.pallas_call(
        kernel,
        out_shape=[
            jax.ShapeDtypeStruct((8, D), f32),
            jax.ShapeDtypeStruct((2 * IMGS, wide), bf16),
        ],
        name="gain_rows",
    )(*sums, *factors, *scales, turn_sums)


def gate_up_grads(normed_ffn, gate_back, up_back, after=()):
    tokens = normed_ffn.shape[0]
    tile = 1024
    tiles = FF // tile

    def kernel(left_ref, gate_ref, up_ref, out_ref):
        step = pl.program_id(0)

        @pl.when(step < tiles)
        def _():
            out_ref[...] = dot_tn(left_ref[...], gate_ref[...]).astype(bf16)

        @pl.when(step >= tiles)
        def _():
            out_ref[...] = dot_tn(left_ref[...], up_ref[...]).astype(bf16)

    return pl.pallas_call(
        ordered(kernel, len(after)),
        grid=(2 * tiles,),
        in_specs=unread(after)
        + [
            whole(normed_ffn.shape),
            pl.BlockSpec((tokens, tile), lambda i: (0, jnp.minimum(i, tiles - 1))),
            pl.BlockSpec((tokens, tile), lambda i: (0, jnp.maximum(i - tiles, 0))),
        ],
        out_specs=pl.BlockSpec((D, tile), lambda i: (0, i)),
        out_shape=jax.ShapeDtypeStruct((D, 2 * FF), bf16),
        compiler_params=pltpu.CompilerParams(vmem_limit_bytes=vmem_bytes),
        cost_estimate=estimate(
            flops=4 * tokens * D * FF, bytes_accessed=4 * D * FF + 4 * tokens * FF, transcendentals=0
        ),
        name="gate_up_grads",
    )(*after, normed_ffn, gate_back, up_back)


def masked_grads(left, right, column, width, place, which, whole_width, offset, into=(), after=()):
    tokens = left.shape[0]
    tile = width if width <= 768 else width // 2
    tiles = width // tile
    masks = place[1][which]
    share = D // len(masks)

    half = len(masks) // 2

    def kernel(left_ref, right_ref, me_ref, *rest):
        kept_ref, sent_ref, held, sems = rest[-4:]
        step = pl.program_id(0)

        def copies(number):
            slot = number % 2
            listed = []
            for index, mask in enumerate(masks):
                low = pl.multiple_of((me_ref[0] ^ mask) * share, share)
                target = kept_ref if index < half else sent_ref
                block = pl.ds(index % half * share, share)
                listed.append(
                    pltpu.make_async_copy(
                        held.at[slot, pl.ds(low, share), :],
                        target.at[block, pl.ds(offset + number * tile, tile)],
                        sems.at[slot, index],
                    )
                )
            return listed

        for number in range(tiles):

            @pl.when(step == number)
            def _():
                if number >= 2:
                    for copy in copies(number - 2):
                        copy.wait()
                held[number % 2] = dot_tn(left_ref[...], right_ref[...]).astype(bf16)
                for copy in copies(number):
                    copy.start()
                if number == tiles - 1:
                    for past in range(max(tiles - 2, 0), tiles):
                        for copy in copies(past):
                            copy.wait()

    return pl.pallas_call(
        ordered(kernel, len(after)),
        grid=(tiles,),
        in_specs=unread(after)
        + [
            whole(left.shape),
            pl.BlockSpec((tokens, tile), lambda i: (0, i + column * tiles)),
            pl.BlockSpec(memory_space=pltpu.SMEM),
        ]
        + unread(into),
        input_output_aliases={len(after) + 3 + index: index for index in range(len(into))},
        out_specs=[pl.BlockSpec(memory_space=pl.ANY)] * 2,
        out_shape=[jax.ShapeDtypeStruct((D // 2, whole_width), bf16)] * 2,
        scratch_shapes=[
            pltpu.VMEM((2, D, tile), bf16),
            pltpu.SemaphoreType.DMA((2, len(masks))),
        ],
        compiler_params=pltpu.CompilerParams(vmem_limit_bytes=vmem_bytes),
        cost_estimate=estimate(
            flops=2 * tokens * D * width,
            bytes_accessed=2 * (D + tokens) * width + 2 * tokens * D,
            transcendentals=0,
        ),
        name="masked_grads",
    )(*after, left, right, place[0], *into)


def third_grads(hidden, ffn_back, place, total, offset, after=()):
    tokens, length = hidden.shape
    width = D // 3
    masks = place[1]
    count = len(masks[0])
    share = length // count
    half = count // 2

    def kernel(left_ref, right_ref, me_ref, *rest):
        targets, held, sems = rest[:6], rest[6], rest[7]
        step = pl.program_id(0)

        def copies(part):
            listed = []
            for index, mask in enumerate(masks[part]):
                low = pl.multiple_of((me_ref[0] ^ mask) * share, share)
                listed.append(
                    pltpu.make_async_copy(
                        held.at[part, pl.ds(low, share), :],
                        targets[2 * part + index // half].at[
                            pl.ds(index % half * share, share), pl.ds(offset, width)
                        ],
                        sems.at[part, index],
                    )
                )
            return listed

        for part in range(3):

            @pl.when(step == part)
            def _():
                held[part] = dot_tn(left_ref[...], right_ref[...]).astype(bf16)
                for copy in copies(part):
                    copy.start()
                if part == 2:
                    for past in range(3):
                        for copy in copies(past):
                            copy.wait()

    results = pl.pallas_call(
        ordered(kernel, len(after)),
        grid=(3,),
        in_specs=unread(after)
        + [
            whole(hidden.shape),
            pl.BlockSpec((tokens, width), lambda i: (0, i)),
            pl.BlockSpec(memory_space=pltpu.SMEM),
        ],
        out_specs=[pl.BlockSpec(memory_space=pl.ANY)] * 6,
        out_shape=[jax.ShapeDtypeStruct((length // 2, total), bf16)] * 6,
        scratch_shapes=[
            pltpu.VMEM((3, length, width), bf16),
            pltpu.SemaphoreType.DMA((3, count)),
        ],
        compiler_params=pltpu.CompilerParams(vmem_limit_bytes=vmem_bytes),
        cost_estimate=estimate(
            flops=2 * tokens * D * length,
            bytes_accessed=2 * (tokens + D) * length + 2 * tokens * D,
            transcendentals=0,
        ),
        name="third_grads",
    )(*after, hidden, ffn_back, place[0])
    return [(results[2 * part], results[2 * part + 1]) for part in range(3)]


def head_lanes(shape, axis, head):
    lane = lax.broadcasted_iota(jnp.int32, shape, axis)
    return (lane >= HD) == (head == 1)


def attend(queries, keys, values, spec_of, width, query_image, key_image):
    length = queries.shape[0]
    pairs = width // LANES
    part = min(1024, length)

    def kernel(q_ref, k_ref, v_ref, qi_ref, ki_ref, out_ref, log_ref):
        key_block = k_ref[...]
        value_turned = v_ref[...].T
        key_parts = []
        value_parts = []
        for head in range(2):
            mine = head_lanes((length, LANES), 1, head)
            key_parts.append(jnp.where(mine, key_block, ki_ref[...]))
            value_parts.append(
                jnp.where(head_lanes((LANES, length), 0, head), value_turned, jnp.ones((), bf16))
            )

        for low in range(0, length, part):
            rows = pl.ds(low, part)
            query = q_ref[rows, :] * jnp.asarray(HD ** (-0.5), bf16)
            scores = []
            for head in range(2):
                mine = head_lanes((part, LANES), 1, head)
                scores.append(
                    dot_nt(key_parts[head], jnp.where(mine, query, qi_ref[rows, :]))
                )
            tops = [jnp.max(score, axis=0, keepdims=True) for score in scores]
            raised = [jnp.exp(score - top).astype(bf16) for score, top in zip(scores, tops)]
            results = [dot_nn(value_parts[head], raised[head]) for head in range(2)]
            turned = []
            for head in range(2):
                lane = HD * (1 - head)
                count = results[head][lane : lane + 1, :]
                turned.append(results[head][head * HD : (head + 1) * HD, :] / count)
                log_ref[0, pl.ds(head, 1), rows] = tops[head] + jnp.log(count)
            out_ref[rows, :] = jnp.concatenate(turned, axis=0).T.astype(bf16)

    return pl.pallas_call(
        kernel,
        grid=(pairs,),
        in_specs=[
            pl.BlockSpec((length, LANES), spec_of(0)),
            pl.BlockSpec((length, LANES), spec_of(1)),
            pl.BlockSpec((length, LANES), spec_of(2)),
            whole(query_image.shape),
            whole(key_image.shape),
        ],
        out_specs=[
            pl.BlockSpec((length, LANES), lambda i: (0, i)),
            pl.BlockSpec((1, 2, length), lambda i: (i, 0, 0)),
        ],
        out_shape=[
            jax.ShapeDtypeStruct((length, width), bf16),
            jax.ShapeDtypeStruct((pairs, 2, length), f32),
        ],
        compiler_params=pltpu.CompilerParams(vmem_limit_bytes=vmem_bytes),
        cost_estimate=estimate(
            flops=16 * pairs * length * length * HD * 4,
            bytes_accessed=8 * length * width,
            transcendentals=2 * pairs * length * length,
        ),
        name="attend",
    )(queries, keys, values, query_image, key_image)


def attend_back(
    queries, keys, values, spec_of, width, attended, grads, log_total, query_image, key_image,
    pairs, first, before, after=(),
):
    length = queries.shape[0]
    part = min(1024, length)
    score_scale = HD ** (-0.5)

    def kernel(
        q_ref, k_ref, v_ref, o_ref, g_ref, log_ref, qi_ref, ki_ref, *rest
    ):
        dq_ref, dk_ref, dv_ref, key_sum, value_sum = rest[-5:]
        key_block = k_ref[...]
        value_block = v_ref[...]
        key_turned = key_block.T
        key_parts = []
        value_parts = []
        for head in range(2):
            mine = head_lanes((length, LANES), 1, head)
            key_parts.append(jnp.where(mine, key_block, ki_ref[...]))
            value_parts.append(jnp.where(mine, value_block, jnp.zeros((), bf16)))
        key_sum[...] = jnp.zeros_like(key_sum)
        value_sum[...] = jnp.zeros_like(value_sum)
        sel_rows = lax.broadcasted_iota(jnp.int32, (8, LANES), 0)
        sel_lanes = lax.broadcasted_iota(jnp.int32, (8, LANES), 1)
        select = jnp.where(
            sel_rows == jnp.where(sel_lanes >= HD, 1, 0), jnp.ones((), f32), jnp.zeros((), f32)
        ).astype(bf16)

        for low in range(0, length, part):
            rows = pl.ds(low, part)
            query = q_ref[rows, :] * jnp.asarray(score_scale, bf16)
            grad = g_ref[rows, :]
            product = grad.astype(f32) * o_ref[rows, :].astype(f32)
            upper = product.astype(bf16)
            lower = (product - upper.astype(f32)).astype(bf16)
            inner = dot_nt(select, upper) + dot_nt(select, lower)
            turned = []
            for head in range(2):
                mine = head_lanes((part, LANES), 1, head)
                scores = dot_nt(key_parts[head], jnp.where(mine, query, qi_ref[rows, :]))
                chances = jnp.exp(scores - log_ref[0, pl.ds(head, 1), rows])
                grad_chances = dot_nt(value_parts[head], grad)
                grad_scores = (chances * (grad_chances - inner[head : head + 1, :])).astype(bf16)
                value_sum[head] += dot_nn(chances.astype(bf16), grad)
                key_sum[head] += dot_nn(grad_scores, query)
                result = dot_nn(key_turned, grad_scores)
                turned.append(result[head * HD : (head + 1) * HD, :])
            dq_ref[rows, :] = (jnp.concatenate(turned, axis=0).T * score_scale).astype(bf16)
        lower_lanes = head_lanes((length, LANES), 1, 0)
        dk_ref[...] = jnp.where(lower_lanes, key_sum[0], key_sum[1]).astype(bf16)
        dv_ref[...] = jnp.where(lower_lanes, value_sum[0], value_sum[1]).astype(bf16)

    column = pl.BlockSpec((length, LANES), lambda i: (0, i + first))
    moved = lambda which: (lambda i: spec_of(which)(i + first))
    held = list(before or [])
    return pl.pallas_call(
        ordered(kernel, len(after)),
        grid=(pairs,),
        in_specs=unread(after)
        + [
            pl.BlockSpec((length, LANES), moved(0)),
            pl.BlockSpec((length, LANES), moved(1)),
            pl.BlockSpec((length, LANES), moved(2)),
            column,
            column,
            pl.BlockSpec((1, 2, length), lambda i: (i + first, 0, 0)),
            whole(query_image.shape),
            whole(key_image.shape),
        ]
        + [pl.BlockSpec(memory_space=pl.ANY)] * len(held),
        input_output_aliases={len(after) + 8 + index: index for index in range(len(held))},
        out_specs=[column] * 3,
        out_shape=[jax.ShapeDtypeStruct((length, width), bf16)] * 3,
        scratch_shapes=[
            pltpu.VMEM((2, length, LANES), f32),
            pltpu.VMEM((2, length, LANES), f32),
        ],
        compiler_params=pltpu.CompilerParams(vmem_limit_bytes=vmem_bytes),
        cost_estimate=estimate(
            flops=40 * pairs * length * length * HD * 4,
            bytes_accessed=16 * length * width,
            transcendentals=2 * pairs * length * length,
        ),
        name="attend_back",
    )(*after, queries, keys, values, attended, grads, log_total, query_image, key_image, *held)


def gate_up_rows(normed, weight):
    tokens = normed.shape[0]
    tile = 512
    tiles = FF // tile

    def kernel(left_ref, gate_weight, up_weight, hidden_ref, gate_ref, up_ref):
        gate = dot_nn(left_ref[...], gate_weight[...])
        up = dot_nn(left_ref[...], up_weight[...])
        hidden_ref[...] = (gate / (1.0 + jnp.exp(-gate)) * up).astype(bf16)
        gate_ref[...] = gate.astype(bf16)
        up_ref[...] = up.astype(bf16)

    out = pl.BlockSpec((tokens, tile), lambda i: (0, i))
    return pl.pallas_call(
        kernel,
        grid=(tiles,),
        in_specs=[
            whole(normed.shape),
            pl.BlockSpec((D, tile), lambda i: (0, i)),
            pl.BlockSpec((D, tile), lambda i: (0, i + tiles)),
        ],
        out_specs=[out] * 3,
        out_shape=[jax.ShapeDtypeStruct((tokens, FF), bf16)] * 3,
        compiler_params=pltpu.CompilerParams(vmem_limit_bytes=vmem_bytes),
        cost_estimate=estimate(
            flops=4 * tokens * D * FF, bytes_accessed=4 * D * FF + 6 * tokens * FF, transcendentals=0
        ),
        name="gate_up_rows",
    )(normed, weight, weight)


def gate_up_back(ffn_back, weight, gate, up, after=()):
    tokens = ffn_back.shape[0]
    tile = 512
    tiles = FF // tile

    def kernel(left_ref, weight_ref, gate_ref, up_ref, gate_back, up_back):
        grad = dot_nt(left_ref[...], weight_ref[...])
        gate_rows = gate_ref[...].astype(f32)
        share = 1.0 / (1.0 + jnp.exp(-gate_rows))
        active = gate_rows * share
        up_back[...] = (grad * active).astype(bf16)
        slope = share + active * (1.0 - share)
        gate_back[...] = (grad * up_ref[...].astype(f32) * slope).astype(bf16)

    column = pl.BlockSpec((tokens, tile), lambda i: (0, i))
    return pl.pallas_call(
        ordered(kernel, len(after)),
        grid=(tiles,),
        in_specs=unread(after)
        + [
            whole(ffn_back.shape),
            pl.BlockSpec((tile, D), lambda i: (i, 0)),
            column,
            column,
        ],
        out_specs=[column] * 2,
        out_shape=[jax.ShapeDtypeStruct((tokens, FF), bf16)] * 2,
        compiler_params=pltpu.CompilerParams(vmem_limit_bytes=vmem_bytes),
        cost_estimate=estimate(
            flops=2 * tokens * D * FF, bytes_accessed=2 * D * FF + 8 * tokens * FF, transcendentals=0
        ),
        name="gate_up_back",
    )(*after, ffn_back, weight, gate, up)


def output_rows(attended, weight, column, embedded, image, post_table, pre_table):
    def body(value, rows, ins, consts, outs, scratch):
        hat = value * inverse_rms(value)
        image_rows = ins[1][rows, :1]
        mixed = ins[0][rows, :] + picked(image_rows, consts[0][...]) * hat
        outs[0][rows, :] = value
        outs[1][rows, :] = mixed
        outs[2][rows, :] = (
            mixed * inverse_rms(mixed) * picked(image_rows, consts[1][...])
        ).astype(bf16)

    return matmul_rows(
        "output_rows", [attended], weight, "nn", 768, [embedded, image], [post_table, pre_table],
        [(D, f32), (D, f32), (D, bf16)], [], body, shape=(D, D), column=column,
    )


def down_rows(hidden, weight, mixed, image, onehot, grad_patches, post_table, out_table, w_final):
    def before(ins, consts, outs, scratch):
        scratch[0][...] = dot_nt(ins[3][...], consts[2][...])

    def body(value, rows, ins, consts, outs, scratch):
        inverse = inverse_rms(value)
        hat = value * inverse
        image_rows = ins[1][rows, :1]
        post = picked(image_rows, consts[0][...])
        final_state = ins[0][rows, :] + post * hat
        centred = final_state - row_mean(final_state)
        spread = inverse_rms(centred)
        levelled = centred * spread
        scale = picked(image_rows, consts[1][...])
        outs[0][rows, :] = (levelled * scale).astype(bf16)
        grad = scratch[0][rows, :]
        scratch[1][rows, :] = grad * levelled
        back = grad * scale
        late = spread * (back - row_mean(back) - levelled * row_mean(back * levelled))
        outs[1][rows, :] = late
        scratch[2][rows, :] = late * hat
        back = late * post
        outs[2][rows, :] = (inverse * (back - hat * row_mean(back * hat))).astype(bf16)

    def after(ins, consts, outs, sums, scratch):
        outs[3][...] = dot_nn(outs[0][...], consts[2][...]).astype(bf16)
        one = ins[2][...]
        sums[0][...] += image_sums(one, scratch[1][...])
        sums[1][...] += image_sums(one, scratch[2][...])

    return matmul_rows(
        "down_rows", [hidden], weight, "nn", 1024, [mixed, image, onehot, grad_patches],
        [post_table, out_table, w_final],
        [(D, bf16), (D, f32), (D, bf16), (PIN, bf16)], [8, 8], body,
        before=before, after=after, block_scratch=[(D, f32)] * 3,
    )


def ffn_back_rows(
    gate_back, up_back, weight, late, mixed, attn_out, image, onehot, post_table, pre_table,
    wait=(),
):
    def body(value, rows, ins, consts, outs, scratch):
        image_rows = ins[3][rows, :1]
        mixed_rows = ins[1][rows, :]
        inverse = inverse_rms(mixed_rows)
        hat = mixed_rows * inverse
        scratch[0][rows, :] = value * hat
        back = value * picked(image_rows, consts[1][...])
        early = ins[0][rows, :] + inverse * (back - hat * row_mean(back * hat))
        outs[0][rows, :] = early
        attn_rows = ins[2][rows, :]
        inverse = inverse_rms(attn_rows)
        hat = attn_rows * inverse
        scratch[1][rows, :] = early * hat
        back = early * picked(image_rows, consts[0][...])
        outs[1][rows, :] = (inverse * (back - hat * row_mean(back * hat))).astype(bf16)

    def after(ins, consts, outs, sums, scratch):
        one = ins[4][...]
        sums[0][...] += image_sums(one, scratch[0][...])
        sums[1][...] += image_sums(one, scratch[1][...])

    return matmul_rows(
        "ffn_back_rows", [gate_back, up_back], weight, "nt", 1024,
        [late, mixed, attn_out, image, onehot], [post_table, pre_table],
        [(D, f32), (D, bf16)], [8, 8], body, after=after, block_scratch=[(D, f32)] * 2,
        wait=wait,
    )


def project_back_rows(
    backs, weight, embedded, late, image, onehot, pre_table, w_embed, wait=()
):
    def body(value, rows, ins, consts, outs, scratch):
        embedded_rows = ins[0][rows, :]
        inverse = inverse_rms(embedded_rows)
        hat = embedded_rows * inverse
        scratch[0][rows, :] = value * hat
        back = value * picked(ins[2][rows, :1], consts[0][...])
        early = inverse * (back - hat * row_mean(back * hat))
        outs[0][rows, :] = (early + ins[1][rows, :]).astype(bf16)

    def after(ins, consts, outs, sums, scratch):
        outs[1][...] = dot_nn(outs[0][...], consts[1][...]).astype(bf16)
        sums[0][...] += image_sums(ins[3][...], scratch[0][...])

    return matmul_rows(
        "project_back_rows", backs, weight, "nt", D,
        [embedded, late, image, onehot], [pre_table, w_embed],
        [(D, bf16), (PIN, bf16)], [8], body, after=after, block_scratch=[(D, f32)], wait=wait,
        shape=(3 * D, D),
    )


def turn_back(grad_q, grad_k, hats, inverses, cosine, sine, gains, after=()):
    tokens = grad_q.shape[0]
    block = min(256, tokens)
    chunk = 64

    def kernel(gq_ref, gk_ref, hat_ref, inv_ref, cos_ref, sin_ref, gain_ref, out_ref, sum_ref):
        @pl.when(pl.program_id(0) == 0)
        def _():
            sum_ref[...] = jnp.zeros_like(sum_ref)

        for which, grad_ref in enumerate((gq_ref, gk_ref)):
            gain = gain_ref[which : which + 1, :]

            total = jnp.zeros((8, D), f32)
            for low in range(0, block, chunk):
                rows = pl.ds(low, chunk)
                first = first_lanes(chunk)
                cos_rows = cos_ref[rows, :]
                sin_rows = sin_ref[rows, :]
                pieces = []
                for lane in range(0, D, LANES):
                    part = grad_ref[rows, lane : lane + LANES].astype(f32)
                    pieces.append(part * cos_rows - swapped(part, first) * sin_rows)
                turned = jnp.concatenate(pieces, axis=1)
                hat = hat_ref[rows, which * D : (which + 1) * D].astype(f32)
                inverse = inv_ref[rows, which * LANES : which * LANES + 1]
                back = turned * gain
                out_ref[rows, which * D : (which + 1) * D] = (
                    inverse * (back - hat * row_mean(back * hat))
                ).astype(bf16)
                total = total + jnp.sum((turned * hat).reshape(chunk // 8, 8, D), axis=0)
            sum_ref[which : which + 1, :] += jnp.sum(total, axis=0, keepdims=True)

    row = lambda cols: pl.BlockSpec((block, cols), lambda i: (i, 0))
    return pl.pallas_call(
        ordered(kernel, len(after)),
        grid=(tokens // block,),
        in_specs=unread(after)
        + [
            row(D), row(D), row(2 * D), row(2 * LANES), row(LANES), row(LANES), whole(gains.shape)
        ],
        out_specs=[row(2 * D), pl.BlockSpec((8, D), lambda i: (0, 0))],
        out_shape=[
            jax.ShapeDtypeStruct((tokens, 2 * D), bf16),
            jax.ShapeDtypeStruct((8, D), f32),
        ],
        compiler_params=pltpu.CompilerParams(vmem_limit_bytes=vmem_bytes),
        cost_estimate=estimate(
            flops=40 * tokens * D, bytes_accessed=12 * tokens * D, transcendentals=0
        ),
        name="turn_back",
    )(*after, grad_q, grad_k, hats, inverses, cosine, sine, gains)


def to_strips(tiles):
    micros = tiles.shape[0]
    count = lax.axis_size("rows")
    parts = count // micros
    me = lax.axis_index("rows")
    slots = []
    for shift in range(micros):
        pairs = [(q, ((q % micros - shift) % micros) * parts + q // micros) for q in range(count)]
        sent = lax.dynamic_index_in_dim(tiles, (me % micros - shift) % micros, 0, keepdims=False)
        if any(a != b for a, b in pairs):
            sent = lax.ppermute(sent, "rows", pairs)
        slots.append(sent)
    stacked = jnp.stack(slots)
    order = (jnp.arange(micros) - me // parts) % micros
    ordered = jnp.concatenate(
        [lax.dynamic_index_in_dim(stacked, order[d], 0) for d in range(micros)], axis=0
    )
    kinds, height, width = ordered.shape[1:]
    return ordered.transpose(1, 0, 2, 3).reshape(kinds, micros * height, width)


def from_strips(strip, micros):
    count = lax.axis_size("rows")
    parts = count // micros
    me = lax.axis_index("rows")
    kinds, height, width = strip.shape
    tiles = strip.reshape(kinds, micros, height // micros, width).transpose(1, 0, 2, 3)
    slots = []
    for shift in range(micros):
        pairs = [(((q % micros - shift) % micros) * parts + q // micros, q) for q in range(count)]
        sent = lax.dynamic_index_in_dim(tiles, (me // parts + shift) % micros, 0, keepdims=False)
        if any(a != b for a, b in pairs):
            sent = lax.ppermute(sent, "rows", pairs)
        slots.append(sent)
    stacked = jnp.stack(slots)
    return jnp.concatenate(
        [
            lax.dynamic_index_in_dim(stacked, (me % micros - m) % micros, 0)
            for m in range(micros)
        ],
        axis=0,
    )


def neighbour_pairs(axis, parts):
    count = lax.axis_size(axis)
    ups = [(i, i + 1) for i in range(count - 1) if (i + 1) % parts != 0]
    return ups, [(b, a) for a, b in ups]


def neighbours(values, axis, dim, parts):
    ups, downs = neighbour_pairs(axis, parts)
    head = lax.slice_in_dim(values, 0, 1, axis=dim)
    tail = lax.slice_in_dim(values, values.shape[dim] - 1, values.shape[dim], axis=dim)
    if len(ups) == 0:
        return jnp.zeros_like(head), jnp.zeros_like(tail)
    return lax.ppermute(tail, axis, ups), lax.ppermute(head, axis, downs)


def sides(parts):
    return (("cols", 1, lax.axis_size("cols")), ("rows", 0, parts))


def window_filter(turned):
    values = jnp.eye(PIN, dtype=bf16).reshape(PIN, CHANNELS, 4, 4)
    return values[:, :, ::-1, ::-1].transpose(1, 0, 2, 3) if turned else values


def extract_patches(strip, parts):
    for axis, dim, span in sides(parts):
        before, after = neighbours(strip, axis, dim + 1, span)
        strip = jnp.concatenate([before, strip, after], axis=dim + 1)
    kinds, height, width = strip.shape
    sets = kinds // CHANNELS
    rows, cols = height // 2 - 1, width // 2 - 1
    windows = lax.conv_general_dilated(
        strip.reshape(sets, CHANNELS, height, width),
        window_filter(False),
        (2, 2),
        "VALID",
        dimension_numbers=("NCHW", "OIHW", "NHWC"),
        preferred_element_type=f32,
    )
    return windows.astype(bf16).reshape(sets, rows * cols, PIN)


def fold_patches(pieces, rows, cols):
    canvas = lax.conv_general_dilated(
        pieces.reshape(1, rows, cols, PIN),
        window_filter(True),
        (1, 1),
        ((3, 3), (3, 3)),
        lhs_dilation=(2, 2),
        dimension_numbers=("NHWC", "OIHW", "NCHW"),
        preferred_element_type=f32,
    )
    return canvas[0]


def share_rims(canvas, parts):
    for axis, dim, span in sides(parts):
        dim += 1
        before, after = neighbours(canvas, axis, dim, span)
        size = canvas.shape[dim]
        middle = list(canvas.shape)
        middle[dim] = size - 4
        canvas = lax.slice_in_dim(canvas, 1, size - 1, axis=dim)
        canvas = canvas + jnp.concatenate([before, jnp.zeros(middle, f32), after], axis=dim)
    return canvas


def strip_layout(heights, seq_rows):
    starts = jnp.cumsum(heights) - heights
    rows_all = jnp.arange(seq_rows, dtype=jnp.int32)
    image_of = jnp.sum((rows_all[:, None] >= starts[None, 1:]).astype(jnp.int32), axis=1)
    start_of = jnp.sum(
        jnp.where(
            image_of[:, None] == jnp.arange(IMGS, dtype=jnp.int32)[None, :], starts[None, :], 0
        ),
        axis=1,
    )
    return (image_of, rows_all - start_of)


def rope_tables(row_place, column):
    quarter = HD // 4
    lane = jnp.arange(LANES, dtype=jnp.int32)
    frequency = 10000.0 ** (-(lane % quarter).astype(f32) / quarter)
    spot = jnp.where((lane % HD < HD // 2)[None, :], row_place[:, None], column[:, None])
    angles = spot.astype(f32) * frequency[None, :]
    sign = jnp.where(lane % 32 < 16, -1.0, 1.0)
    return (jnp.cos(angles), jnp.sin(angles) * sign[None, :])


def gather_all(shard):
    return lax.all_gather(shard, ALL, axis=0, tiled=True)


def scatter_all(part):
    return lax.psum_scatter(part, ALL, scatter_dimension=0, tiled=True)


def bits_of(axis):
    return lax.axis_size(axis).bit_length() - 1


def orders():
    first = [("fsdp", bit) for bit in range(bits_of("fsdp"))]
    main = [("cols", 0), ("rows", 0), ("cols", 1)]
    rest = [("rows", bit) for bit in range(1, bits_of("rows"))]
    rest += [("cols", bit) for bit in range(2, bits_of("cols"))]
    return [first + main[turn:] + main[:turn] + rest for turn in range(3)]


def block_masks(order):
    base = {"fsdp": 0, "cols": bits_of("fsdp"), "rows": bits_of("fsdp") + bits_of("cols")}
    steps = len(order)
    return [
        sum(
            ((index >> (steps - 1 - step)) & 1) << (base[axis] + bit)
            for step, (axis, bit) in enumerate(order)
        )
        for index in range(1 << steps)
    ]


def swap(values, axis, bit):
    return lax.ppermute(values, axis, [(i, i ^ (1 << bit)) for i in range(lax.axis_size(axis))])


class Gather:
    def __init__(self, values, picks):
        self.steps = [list(reversed(order)) for order in picks]
        self.held = list(values)
        self.step = 0
        self.received = []

    def start(self):
        self.received = [
            swap(value, *self.steps[k][self.step]) for k, value in enumerate(self.held)
        ]

    def finish(self):
        self.step += 1
        if self.done():
            self.held = list(zip(self.held, self.received))
        else:
            self.held = [jnp.concatenate(pair, axis=0) for pair in zip(self.held, self.received)]

    def done(self):
        return self.step == len(self.steps[0])


class Scatter:
    def __init__(self, halves, picks):
        self.steps = picks
        self.terms = [[kept] for kept, _ in halves]
        self.sent = [sent for _, sent in halves]
        self.kinds = [kept.dtype for kept, _ in halves]
        self.step = 0
        self.received = []

    def total(self, values):
        return sum(value.astype(f32) for value in values)

    def sent_next(self):
        sent = []
        for terms, kind in zip(self.terms, self.kinds):
            half = terms[0].shape[0] // 2
            sent.append(self.total([term[half:] for term in terms]).astype(kind))
        return sent

    def start(self):
        if self.step > 0:
            self.sent = self.sent_next()
            self.terms = [[term[: term.shape[0] // 2] for term in terms] for terms in self.terms]
        self.received = [
            swap(sent, *order[self.step]) for sent, order in zip(self.sent, self.steps)
        ]

    def finish(self):
        self.step += 1
        self.terms = [terms + [value] for terms, value in zip(self.terms, self.received)]

    def done(self):
        return self.step == len(self.steps[0])

    def sums(self):
        return [self.total(values) for values in self.terms]


def halves_of(values):
    half = values.shape[0] // 2
    return values[:half], values[half:]


def wait_for(chain, *others):
    chain.received[0] = held_until(chain.received[0], *others)


def step_all(value, *chains):
    for chain in chains:
        wait_for(chain, value)
    go_on(*chains)


def arrived(*chains):
    return tuple(value for chain in chains for value in chain.received)


def go_on(*chains):
    for chain in chains:
        chain.finish()
        if not chain.done():
            chain.start()


def exchange_heads(parts, micros):
    groups = [[m * parts + s for s in range(parts)] for m in range(micros)]

    def spread(values):
        return lax.all_to_all(
            values, "rows", split_axis=1, concat_axis=0, tiled=True, axis_index_groups=groups
        )

    def collect(values):
        return lax.all_to_all(
            values, "rows", split_axis=0, concat_axis=1, tiled=True, axis_index_groups=groups
        )

    return spread, collect


def shards(
    latent,
    time_embed,
    image_rows,
    pred_grad,
    embed_weight,
    adaptive_weight,
    project_weight,
    output_weight,
    gate_up_weight,
    down_weight,
    final_weight,
    norm_gains,
):
    micros = latent.shape[0]
    row_devices = lax.axis_size("rows")
    parts = row_devices // micros
    row_index = lax.axis_index("rows")
    micro, piece = row_index // parts, row_index % parts
    device = (row_index * lax.axis_size("cols") + lax.axis_index("cols")) * lax.axis_size(
        "fsdp"
    ) + lax.axis_index("fsdp")
    rows = latent.shape[3] // 2 * micros
    cols = latent.shape[4] // 2
    tokens = rows * cols
    seq_rows = rows * parts
    length = seq_rows * cols

    devices = lax.axis_size(ALL)
    share = D // devices
    near = share % 16 == 0 and FF // devices % LANES == 0
    picks = orders()
    place = None
    if near:
        place = (device.astype(jnp.int32).reshape(1), [block_masks(order) for order in picks])

    tiles = jnp.concatenate([latent[:, 0], pred_grad[:, 0]], axis=1)
    small = jnp.concatenate(
        [
            embed_weight,
            final_weight,
            norm_gains,
            jnp.zeros((norm_gains.shape[0], 2 * LANES - 2 * PIN - 6), bf16),
        ],
        axis=1,
    )
    temb = lax.dynamic_index_in_dim(time_embed, micro, 0, keepdims=False)[0, 0]
    condition = jax.nn.silu(temb).astype(bf16)
    rows_held = adaptive_weight.shape[0]
    if near:
        wide = condition.reshape(-1, 2 * LANES)
        side = Gather([jnp.concatenate([small, wide], axis=0)], picks[:1])
        side.start()
        while not side.done():
            go_on(side)
        small_pairs = side.held
        both = jnp.concatenate(side.held[0], axis=0)
        both = both.reshape(devices, share + wide.shape[0], 2 * LANES)
        conditions = both[:, share:].reshape(devices * IMGS, condition.shape[1])
        conditions = lax.dynamic_slice_in_dim(conditions, device * rows_held, rows_held, axis=1)
        per_image = dot_nn(conditions, adaptive_weight)
        side = Scatter([halves_of(per_image)], picks[:1])
        side.start()
        while not side.done():
            go_on(side)
        joined = gather_all(jnp.concatenate([project_weight, output_weight], axis=1))
        w_project = joined
        w_output = joined[:, 3 * D :]
        w_down = gather_all(down_weight)
        per_image = side.sums()[0]
        source = jnp.asarray(place[1][0], jnp.int32)
        count = len(picks[0])
        small = arrange(small_pairs, place, share)
    else:
        small = gather_all(small)
        conditions = gather_all(condition)
        conditions = lax.dynamic_slice_in_dim(conditions, device * rows_held, rows_held, axis=1)
        per_image = scatter_all(dot_nn(conditions, adaptive_weight))
        w_project = gather_all(project_weight)
        w_output = gather_all(output_weight)
        joined = w_output
        w_down = gather_all(down_weight)
    w_embed = small[:, :PIN]
    w_final = small[:, PIN : 2 * PIN]
    gains = small[:, 2 * PIN : 2 * PIN + 6].astype(f32).T

    w_gate_up = gather_all(gate_up_weight)

    patches, grad_patches = extract_patches(to_strips(tiles), parts)

    heights = lax.dynamic_index_in_dim(image_rows, micro, 0, keepdims=False)[0, 0]
    row_image, row_place = strip_layout(heights, seq_rows)
    first_row = piece * rows
    my_image = lax.dynamic_slice_in_dim(row_image, first_row, rows)
    my_place = lax.dynamic_slice_in_dim(row_place, first_row, rows)
    token_image = jnp.repeat(my_image, cols)
    cosine, sine = rope_tables(
        jnp.repeat(my_place, cols), jnp.tile(jnp.arange(cols, dtype=jnp.int32), rows)
    )
    image = jnp.broadcast_to(token_image[:, None], (tokens, LANES))
    onehot = (token_image[None, :] == jnp.arange(8, dtype=jnp.int32)[:, None]).astype(bf16)
    strip_image = jnp.repeat(row_image, cols)
    head_lane = jnp.arange(LANES, dtype=jnp.int32)[None, :] % HD
    same = strip_image[:, None] == head_lane
    query_image = jnp.where(same, -mask_level, 0.0).astype(bf16)
    key_image = jnp.where(same | (head_lane >= IMGS), 0.0, mask_level).astype(bf16)

    modulation = per_image.reshape(IMGS, 5, D)
    scale_attn = 1.0 + modulation[:, 0]
    gate_attn = jnp.tanh(modulation[:, 1])
    scale_ffn = 1.0 + modulation[:, 2]
    gate_ffn = jnp.tanh(modulation[:, 3])
    scale_out = 1.0 + modulation[:, 4]
    table = lambda values: jnp.concatenate([values, values], axis=0)
    attn_pre = table(scale_attn * gains[0])
    attn_post = table(gate_attn * gains[3])
    ffn_pre = table(scale_ffn * gains[4])
    ffn_post = table(gate_ffn * gains[5])
    out_scale = table(scale_out)
    turn_gains = jnp.concatenate([gains[1:3], jnp.zeros((6, D), f32)], axis=0)
    factors = [
        jnp.broadcast_to(gains[0], (IMGS, D)),
        (1.0 - gate_attn * gate_attn) * gains[3],
        jnp.broadcast_to(gains[4], (IMGS, D)),
        (1.0 - gate_ffn * gate_ffn) * gains[5],
        jnp.ones((IMGS, D), f32),
    ]

    embedded, normed, projected, hats, inverses = project_rows(
        patches, image, cosine, sine, w_embed, attn_pre, w_project, turn_gains
    )
    if parts == 1:
        pairs = D // LANES
        heads = (projected, projected, projected)
        spec_of = lambda which: (lambda i: (0, which * pairs + i))
        width = D
    else:
        spread, collect = exchange_heads(parts, micros)
        heads = tuple(spread(projected[:, w * D : (w + 1) * D]) for w in range(3))
        spec_of = lambda which: (lambda i: (0, i))
        width = D // parts
    attended_heads, log_total = attend(*heads, spec_of, width, query_image, key_image)
    attended = attended_heads if parts == 1 else collect(attended_heads)
    attn_out, mixed, normed_ffn = output_rows(
        attended, joined, 3 if near else 0, embedded, image, attn_post, ffn_pre
    )
    hidden, gate, up = gate_up_rows(normed_ffn, w_gate_up)
    final, late, ffn_back, pieces, sum_out, sum_ffn_post = down_rows(
        hidden, w_down, mixed, image, onehot, grad_patches, ffn_post, out_scale, w_final
    )
    if near:
        down_parts = third_grads(hidden, ffn_back, place, D // 3, 0)
        down_chain = Scatter(down_parts, picks)
        down_chain.start()
        gate_back, up_back = gate_up_back(
            ffn_back, w_down, gate, up, after=[part[0] for part in down_parts]
        )
        waits = arrived(down_chain)
        step_all(gate_back, down_chain)
        waits += tuple(down_chain.sent)
        gate_up_grad = gate_up_grads(normed_ffn, gate_back, up_back, after=waits)
        gate_up_share = scatter_all(gate_up_grad)
        waits = arrived(down_chain) + (gate_up_grad,)
        step_all(gate_up_grad, down_chain)
        waits += tuple(down_chain.sent)
    else:
        down_share = scatter_all(dot_tn(hidden, ffn_back).astype(bf16))
        gate_back, up_back = gate_up_back(ffn_back, w_down, gate, up)
        gate_up_share = scatter_all(gate_up_grads(normed_ffn, gate_back, up_back))
        waits = ()
    early, attn_back, sum_ffn_pre, sum_attn_post = ffn_back_rows(
        gate_back, up_back, w_gate_up, late, mixed, attn_out, image, onehot, attn_post, ffn_pre,
        wait=waits,
    )
    grad_attended = dot_nt(attn_back, w_output).astype(bf16)
    if parts > 1:
        grad_attended = spread(grad_attended)
    back = partial(
        attend_back,
        *heads, spec_of, width, attended_heads, grad_attended, log_total, query_image, key_image,
    )
    if near:
        group = width // LANES // 2
        waits = arrived(down_chain)
        step_all(grad_attended, down_chain)
        waits += tuple(down_chain.sent)
        grads = back(width // LANES, 0, None, after=waits)
    else:
        grads = back(width // LANES, 0, None)
    if parts > 1:
        grads = tuple(collect(grad) for grad in grads)
    grad_q, grad_k, grad_v = grads
    waits = ()
    if near:
        waits = arrived(down_chain)
        step_all(grad_q, down_chain)
        waits += tuple(down_chain.sent)
    turned, sum_turn = turn_back(
        grad_q, grad_k, hats, inverses, cosine, sine, turn_gains, after=waits
    )
    waits = ()
    if near:
        side_width = D // 3
        grad_parts = third_grads(
            attended, attn_back, place, D + side_width, D, after=(grads[0],)
        )
        for k, (back_values, column) in enumerate(((turned, 0), (turned, 1), (grad_v, 0))):
            grad_parts[k] = masked_grads(
                normed, back_values, column, D, place, k, D + side_width, 0, into=grad_parts[k]
            )
        main = Scatter(grad_parts, picks)
        main.start()
        pieces = held_until(pieces, grad_parts[1][0])
    folded = fold_patches(pieces, rows, cols)
    if near:
        waits = arrived(down_chain) + tuple(part[0] for part in grad_parts) + (folded,)
    embed_back, grad_pieces, sum_attn_pre = project_back_rows(
        [turned, grad_v], w_project, embedded, early, image, onehot, attn_pre, w_embed, wait=waits
    )
    if near:
        while not down_chain.done():
            go_on(down_chain)
        down_share = jnp.concatenate(down_chain.sums(), axis=1)
        if WAIT_FOR_GATE_UP:
            wait_for(main, gate_up_share)
        main.finish()
        first_sent = main.sent_next()
        embed_back = held_until(embed_back, *first_sent[1:])
        sum_attn_pre = held_until(sum_attn_pre, *first_sent[1:])
    gain_grads, grad_modulation = gain_rows(
        [sum_attn_pre, sum_attn_post, sum_ffn_pre, sum_ffn_post, sum_out], factors,
        [scale_attn, gate_attn, scale_ffn, gate_ffn], sum_turn,
    )
    if near:
        side = Scatter(
            [small_grads_near(embed_back, patches, final, grad_patches, gain_grads, place)],
            picks[:1],
        )
        side.start()
        side.finish()
        main.terms[0] = [
            jnp.concatenate([large, tiny.astype(bf16)], axis=1)
            for large, tiny in zip(main.terms[0], side.terms[0])
        ]
        main.start()
        grad_modulation = held_until(grad_modulation, main.received[1])
        spread_sums = Gather([grad_modulation], picks[:1])
        spread_sums.start()
        grad_pieces = held_until(grad_pieces, main.received[1])
        while not main.done():
            go_on(main)
        while not spread_sums.done():
            go_on(spread_sums)
        grad_modulations = jnp.concatenate(spread_sums.held[0], axis=0)
        held = main.sums()
        project_share = jnp.concatenate([value[:, :D] for value in held], axis=1)
        output_share = jnp.concatenate([value[:, D : D + side_width] for value in held], axis=1)
        small_share = held[0][:, D + side_width :]
    else:
        grad_modulations = gather_all(grad_modulation)
        small_grads = jnp.concatenate(
            [dot_tn(embed_back, patches), dot_tn(final, grad_patches), gain_grads.T], axis=1
        )
        small_share = scatter_all(
            jnp.pad(small_grads, ((0, 0), (0, 2 * LANES - small_grads.shape[1])))
        )
        project_back = jnp.concatenate([turned, grad_v], axis=1)
        project_share = scatter_all(dot_tn(normed, project_back).astype(bf16))
        output_share = scatter_all(dot_tn(attended, attn_back).astype(bf16))
    prediction = from_strips(share_rims(folded, parts), micros)
    latent_grad = from_strips(
        share_rims(fold_patches(grad_pieces, rows, cols), parts), micros
    )

    spaced = jnp.pad(
        conditions.reshape(devices, IMGS, rows_held), ((0, 0), (0, IMGS), (0, 0))
    )
    adaptive_share = jnp.concatenate(
        [
            dot_tn(values.reshape(2 * devices * IMGS, rows_held), grad_modulations)
            for values in (spaced, jnp.roll(spaced, IMGS, axis=1))
        ],
        axis=1,
    )
    return (
        prediction[:, None],
        latent_grad[:, None],
        small_share[:, :PIN],
        adaptive_share,
        project_share.astype(f32),
        output_share.astype(f32),
        gate_up_share.astype(f32),
        down_share.astype(f32),
        small_share[:, PIN : 2 * PIN],
        small_share[:, 2 * PIN : 2 * PIN + 6],
    )


def solution(mesh):
    canvas = P(None, "fsdp", None, "rows", "cols")
    weight = P(ALL, None)
    return jax.shard_map(
        shards,
        mesh=mesh,
        in_specs=(canvas, P(None, "fsdp", "cols", None, None), P(None, "fsdp", "cols", None), canvas)
        + (weight,) * 8,
        out_specs=(canvas, canvas) + (weight,) * 8,
        check_vma=False,
    )
```

```python
from functools import partial

import jax
import jax.numpy as jnp
from jax import lax
from jax.experimental import pallas as pl
from jax.experimental.pallas import tpu as pltpu
from jax.sharding import PartitionSpec as P

D = 1536
HEADS = 24
HD = 64
FF = 4096
CHANNELS = 4
PIN = 64
IMGS = 4
CELL = 16
LANES = 128
ALL = ("rows", "cols", "fsdp")

epsilon = 1e-06
highest = lax.Precision.HIGHEST
mask_level = 256.0
f32 = jnp.float32
bf16 = jnp.bfloat16
vmem_bytes = 60 * 1024 * 1024
SHRINK = 2
WAIT_FOR_GATE_UP = False


def estimate(flops, bytes_accessed, transcendentals):
    return pl.CostEstimate(
        flops=flops // SHRINK, bytes_accessed=bytes_accessed // SHRINK, transcendentals=0
    )


def ordered(kernel, count):
    return lambda *refs: kernel(*refs[count:])


def unread(arrays):
    return [pl.BlockSpec(memory_space=pl.ANY)] * len(arrays)


def held_until(value, *others):
    return pl.pallas_call(
        lambda *refs: None,
        in_specs=unread((value,) + others),
        out_specs=pl.BlockSpec(memory_space=pl.ANY),
        out_shape=jax.ShapeDtypeStruct(value.shape, value.dtype),
        input_output_aliases={0: 0},
        name="held_until",
    )(value, *others)


def dot_nn(left, right):
    return lax.dot_general(left, right, (((1,), (0,)), ((), ())), preferred_element_type=f32)


def dot_nt(left, right):
    return lax.dot_general(left, right, (((1,), (1,)), ((), ())), preferred_element_type=f32)


def dot_tn(left, right):
    return lax.dot_general(left, right, (((0,), (0,)), ((), ())), preferred_element_type=f32)


def row_mean(values):
    return jnp.mean(values, axis=-1, keepdims=True)


def inverse_rms(values):
    return lax.rsqrt(row_mean(values * values) + epsilon)


def whole(shape):
    zeros = (0,) * len(shape)
    return pl.BlockSpec(shape, lambda i: zeros, pipeline_mode=pl.Buffered(1))


def picked(image, table):
    choice = table[IMGS - 1 : IMGS, :]
    for index in range(IMGS - 2, -1, -1):
        choice = jnp.where(image == index, table[index : index + 1, :], choice)
    return choice


def image_sums(onehot, product):
    upper = product.astype(bf16)
    lower = (product - upper.astype(f32)).astype(bf16)
    return dot_nn(onehot, upper) + dot_nn(onehot, lower)


def matmul_rows(
    name, lefts, weight, kind, depth_tile, row_ins, consts, row_outs, sum_rows, chunk_body,
    before=None, after=None, block_scratch=(), wait=(), shape=None, column=0,
):
    tokens = lefts[0].shape[0]
    depth, width = shape or (weight.shape if kind == "nn" else weight.shape[::-1])
    block = min(256, tokens)
    chunk = 64
    tiles = depth // depth_tile
    blocks = tokens // block
    counts = (len(lefts), len(row_ins), len(consts), len(row_outs), len(sum_rows))
    ends = []
    for left in lefts:
        ends.append((ends[-1] if ends else 0) + left.shape[1] // depth_tile)
    starts = [0] + ends[:-1]

    def kernel(*refs):
        refs = list(refs)
        take = lambda n: [refs.pop(0) for _ in range(n)]
        left_refs = take(counts[0])
        weight_ref = take(1)[0]
        in_refs, const_refs = take(counts[1]), take(counts[2])
        out_refs, sum_refs = take(counts[3]), take(counts[4])
        total = refs.pop(0)
        scratch = refs
        step = pl.program_id(0)
        product = dot_nn if kind == "nn" else dot_nt

        @pl.when(step == 0)
        def _():
            total[...] = product(left_refs[0][...], weight_ref[...])
            for ref in sum_refs:
                ref[...] = jnp.zeros_like(ref)

        for left_ref, low, high in zip(left_refs, starts, ends):

            @pl.when((step >= max(low, 1)) & (step < high))
            def _():
                total[...] += product(left_ref[...], weight_ref[...])

        @pl.when(step >= tiles)
        def _():
            start = pl.multiple_of((step - tiles) * block, block)
            if before is not None:
                before(in_refs, const_refs, out_refs, scratch)
            for low in range(0, block, chunk):
                chunk_body(
                    total[pl.ds(pl.multiple_of(start + low, chunk), chunk), :],
                    pl.ds(low, chunk), in_refs, const_refs, out_refs, scratch,
                )
            if after is not None:
                after(in_refs, const_refs, out_refs, sum_refs, scratch)

    def row_map(i):
        return (jnp.maximum(i - tiles, 0), 0)

    def col_map(i):
        return (0, jnp.maximum(i - tiles, 0))

    def left_map(low, high):
        return lambda i: (0, jnp.clip(i - low, 0, high - low - 1))

    if kind == "nn":
        weight_spec = pl.BlockSpec(
            (depth_tile, width), lambda i: (jnp.minimum(i, tiles - 1), column)
        )
    else:
        weight_spec = pl.BlockSpec((width, depth_tile), lambda i: (0, jnp.minimum(i, tiles - 1)))
    in_specs = [
        pl.BlockSpec((tokens, depth_tile), left_map(low, high)) for low, high in zip(starts, ends)
    ]
    in_specs.append(weight_spec)
    for array in row_ins:
        if array.shape[0] == tokens:
            in_specs.append(pl.BlockSpec((block, array.shape[1]), row_map))
        else:
            in_specs.append(pl.BlockSpec((array.shape[0], block), col_map))
    in_specs += [whole(array.shape) for array in consts]
    out_specs = [pl.BlockSpec((block, cols), row_map) for cols, _ in row_outs]
    out_specs += [pl.BlockSpec((count, width), lambda i: (0, 0)) for count in sum_rows]
    out_shape = [jax.ShapeDtypeStruct((tokens, cols), kind_) for cols, kind_ in row_outs]
    out_shape += [jax.ShapeDtypeStruct((count, width), f32) for count in sum_rows]
    return pl.pallas_call(
        ordered(kernel, len(wait)),
        grid=(tiles + blocks,),
        in_specs=unread(wait) + in_specs,
        out_specs=out_specs,
        out_shape=out_shape,
        scratch_shapes=[pltpu.VMEM((tokens, width), f32)]
        + [pltpu.VMEM((block, cols), kind_) for cols, kind_ in block_scratch],
        compiler_params=pltpu.CompilerParams(vmem_limit_bytes=vmem_bytes),
        cost_estimate=estimate(
            flops=2 * tokens * width * depth,
            bytes_accessed=2 * (width * depth + tokens * depth) + 8 * tokens * width,
            transcendentals=0,
        ),
        name=name,
    )(*wait, *lefts, weight, *row_ins, *consts)


def swapped(values, first):
    return jnp.where(first, pltpu.roll(values, LANES - 16, 1), pltpu.roll(values, 16, 1))


def first_lanes(rows):
    lane = lax.broadcasted_iota(jnp.int32, (rows, LANES), 1)
    return lax.rem(lane, 32) < 16


def project_rows(patches, image, cosine, sine, w_embed, pre_table, w_project, gains):
    tokens = patches.shape[0]
    chunk = min(128, tokens)
    tile = 256
    blocks = D // tile

    def kernel(
        patches_ref, image_ref, cos_ref, sin_ref, embed_ref, pre_ref, weight_ref, gain_ref,
        embedded_ref, normed_ref, out_ref, hat_ref, inverse_ref, total,
    ):
        step = pl.program_id(0)

        @pl.when(step == 0)
        def _():
            total[...] = dot_nt(patches_ref[...], embed_ref[...])

            for low in range(0, tokens, chunk):
                rows = pl.ds(low, chunk)
                value = total[rows, :]
                embedded_ref[rows, :] = value
                normed_ref[rows, :] = (
                    value * inverse_rms(value) * picked(image_ref[rows, :1], pre_ref[...])
                ).astype(bf16)

        for index in range(blocks):
            cols = slice(index * tile, (index + 1) * tile)
            total[:, cols] = dot_nn(normed_ref[...], weight_ref[:, cols])

        @pl.when(step < 2)
        def _():
            gain = gain_ref[pl.ds(step, 1), :]

            for low in range(0, tokens, chunk):
                rows = pl.ds(low, chunk)
                value = total[rows, :]
                inverse = inverse_rms(value)
                hat = value * inverse
                hat_ref[rows, :] = hat.astype(bf16)
                inverse_ref[rows, :] = jnp.broadcast_to(inverse, (chunk, LANES))
                scaled = hat * gain
                first = first_lanes(chunk)
                cos_rows = cos_ref[rows, :]
                sin_rows = sin_ref[rows, :]
                for lane in range(0, D, LANES):
                    part = scaled[:, lane : lane + LANES]
                    turned = part * cos_rows + swapped(part, first) * sin_rows
                    out_ref[rows, lane : lane + LANES] = turned.astype(bf16)

        @pl.when(step == 2)
        def _():
            out_ref[...] = total[...].astype(bf16)

    return pl.pallas_call(
        kernel,
        grid=(3,),
        in_specs=[
            whole(patches.shape),
            whole(image.shape),
            whole(cosine.shape),
            whole(sine.shape),
            whole(w_embed.shape),
            whole(pre_table.shape),
            pl.BlockSpec((D, D), lambda i: (0, i)),
            whole(gains.shape),
        ],
        out_specs=[
            pl.BlockSpec((tokens, D), lambda i: (0, 0), pipeline_mode=pl.Buffered(1)),
            pl.BlockSpec((tokens, D), lambda i: (0, 0), pipeline_mode=pl.Buffered(1)),
            pl.BlockSpec((tokens, D), lambda i: (0, i)),
            pl.BlockSpec((tokens, D), lambda i: (0, jnp.minimum(i, 1))),
            pl.BlockSpec((tokens, LANES), lambda i: (0, jnp.minimum(i, 1))),
        ],
        out_shape=[
            jax.ShapeDtypeStruct((tokens, D), f32),
            jax.ShapeDtypeStruct((tokens, D), bf16),
            jax.ShapeDtypeStruct((tokens, 3 * D), bf16),
            jax.ShapeDtypeStruct((tokens, 2 * D), bf16),
            jax.ShapeDtypeStruct((tokens, 2 * LANES), f32),
        ],
        scratch_shapes=[pltpu.VMEM((tokens, D), f32)],
        compiler_params=pltpu.CompilerParams(vmem_limit_bytes=vmem_bytes),
        cost_estimate=estimate(
            flops=6 * tokens * D * D, bytes_accessed=6 * D * D + 24 * tokens * D, transcendentals=0
        ),
        name="project_rows",
    )(patches, image, cosine, sine, w_embed, pre_table, w_project, gains)


def arrange(pairs, place, used=None):
    count = len(pairs)
    devices = len(place[1][0])
    half = devices // 2
    stride = pairs[0][0].shape[0] // half
    share = stride if used is None else used
    width = pairs[0][0].shape[1]

    def kernel(*refs):
        me_ref, out_ref, sems = refs[2 * count :]
        step = pl.program_id(0)
        for part in range(count):

            @pl.when(step == part)
            def _():
                listed = []
                for index, mask in enumerate(place[1][part]):
                    low = pl.multiple_of((me_ref[0] ^ mask) * share, share)
                    listed.append(
                        pltpu.make_async_copy(
                            refs[2 * part + index // half].at[
                                pl.ds(index % half * stride, share), :
                            ],
                            out_ref.at[pl.ds(low, share), :],
                            sems.at[index],
                        )
                    )
                for copy in listed:
                    copy.start()
                for copy in listed:
                    copy.wait()

    return pl.pallas_call(
        kernel,
        grid=(count,),
        in_specs=[pl.BlockSpec(memory_space=pl.ANY)] * (2 * count)
        + [pl.BlockSpec(memory_space=pltpu.SMEM)],
        out_specs=pl.BlockSpec((devices * share, width), lambda i: (0, i)),
        out_shape=jax.ShapeDtypeStruct((devices * share, count * width), bf16),
        scratch_shapes=[pltpu.SemaphoreType.DMA((devices,))],
        compiler_params=pltpu.CompilerParams(vmem_limit_bytes=vmem_bytes),
        cost_estimate=estimate(
            flops=0, bytes_accessed=4 * devices * share * count * width, transcendentals=0
        ),
        name="arrange",
    )(*[value for pair in pairs for value in pair], place[0])


def small_grads_near(embed_back, patches, final, grad_patches, rows, place):
    masks = place[1][0]
    share = D // len(masks)
    half = len(masks) // 2

    def kernel(e_ref, p_ref, f_ref, g_ref, rows_ref, me_ref, kept_ref, sent_ref, held, sems):
        held[:, :PIN] = dot_tn(e_ref[...], p_ref[...])
        held[:, PIN : 2 * PIN] = dot_tn(f_ref[...], g_ref[...])
        tall = jnp.concatenate([rows_ref[...], jnp.zeros((LANES - 8, D), f32)], axis=0)
        held[:, LANES:] = tall.T
        listed = []
        for index, mask in enumerate(masks):
            low = pl.multiple_of((me_ref[0] ^ mask) * share, share)
            target = kept_ref if index < half else sent_ref
            listed.append(
                pltpu.make_async_copy(
                    held.at[pl.ds(low, share), :],
                    target.at[pl.ds(index % half * share, share), :],
                    sems.at[index],
                )
            )
        for copy in listed:
            copy.start()
        for copy in listed:
            copy.wait()

    return pl.pallas_call(
        kernel,
        in_specs=[pl.BlockSpec(memory_space=pltpu.VMEM)] * 5
        + [pl.BlockSpec(memory_space=pltpu.SMEM)],
        out_specs=[pl.BlockSpec(memory_space=pl.ANY)] * 2,
        out_shape=[jax.ShapeDtypeStruct((D // 2, 2 * LANES), f32)] * 2,
        scratch_shapes=[
            pltpu.VMEM((D, 2 * LANES), f32),
            pltpu.SemaphoreType.DMA((len(masks),)),
        ],
        compiler_params=pltpu.CompilerParams(vmem_limit_bytes=vmem_bytes),
        cost_estimate=estimate(
            flops=4 * patches.shape[0] * D * PIN, bytes_accessed=8 * patches.shape[0] * D,
            transcendentals=0,
        ),
        name="small_grads_near",
    )(embed_back, patches, final, grad_patches, rows, place[0])


def gain_rows(sums, factors, scales, turn_sums):
    wide = 5 * D // 2

    def kernel(*refs):
        sum_refs, factor_refs = refs[:5], refs[5:10]
        scale_refs, turn_ref, rows_ref, out_ref = refs[10:14], refs[14], refs[15], refs[16]
        rows_ref[...] = jnp.zeros_like(rows_ref)
        for spot, index in enumerate((0, 3, 4, 5)):
            rows_ref[index : index + 1, :] = jnp.sum(
                scale_refs[spot][...] * sum_refs[spot][:IMGS, :], axis=0, keepdims=True
            )
        rows_ref[1:3, :] = turn_ref[0:2, :]
        flat = [factor_refs[k][...] * sum_refs[k][:IMGS, :] for k in range(5)]
        middle = wide - 2 * D
        out_ref[:IMGS, :] = jnp.concatenate(flat[:2] + [flat[2][:, :middle]], axis=1).astype(bf16)
        out_ref[IMGS:, :] = jnp.concatenate([flat[2][:, middle:]] + flat[3:], axis=1).astype(bf16)

    return pl.pallas_call(
        kernel,
        out_shape=[
            jax.ShapeDtypeStruct((8, D), f32),
            jax.ShapeDtypeStruct((2 * IMGS, wide), bf16),
        ],
        name="gain_rows",
    )(*sums, *factors, *scales, turn_sums)


def gate_up_grads(normed_ffn, gate_back, up_back, after=()):
    tokens = normed_ffn.shape[0]
    tile = 1024
    tiles = FF // tile

    def kernel(left_ref, gate_ref, up_ref, out_ref):
        step = pl.program_id(0)

        @pl.when(step < tiles)
        def _():
            out_ref[...] = dot_tn(left_ref[...], gate_ref[...]).astype(bf16)

        @pl.when(step >= tiles)
        def _():
            out_ref[...] = dot_tn(left_ref[...], up_ref[...]).astype(bf16)

    return pl.pallas_call(
        ordered(kernel, len(after)),
        grid=(2 * tiles,),
        in_specs=unread(after)
        + [
            whole(normed_ffn.shape),
            pl.BlockSpec((tokens, tile), lambda i: (0, jnp.minimum(i, tiles - 1))),
            pl.BlockSpec((tokens, tile), lambda i: (0, jnp.maximum(i - tiles, 0))),
        ],
        out_specs=pl.BlockSpec((D, tile), lambda i: (0, i)),
        out_shape=jax.ShapeDtypeStruct((D, 2 * FF), bf16),
        compiler_params=pltpu.CompilerParams(vmem_limit_bytes=vmem_bytes),
        cost_estimate=estimate(
            flops=4 * tokens * D * FF, bytes_accessed=4 * D * FF + 4 * tokens * FF, transcendentals=0
        ),
        name="gate_up_grads",
    )(*after, normed_ffn, gate_back, up_back)


def masked_grads(left, right, column, width, place, which, whole_width, offset, into=(), after=()):
    tokens = left.shape[0]
    tile = width if width <= 768 else width // 2
    tiles = width // tile
    masks = place[1][which]
    share = D // len(masks)

    half = len(masks) // 2

    def kernel(left_ref, right_ref, me_ref, *rest):
        kept_ref, sent_ref, held, sems = rest[-4:]
        step = pl.program_id(0)

        def copies(number):
            slot = number % 2
            listed = []
            for index, mask in enumerate(masks):
                low = pl.multiple_of((me_ref[0] ^ mask) * share, share)
                target = kept_ref if index < half else sent_ref
                block = pl.ds(index % half * share, share)
                listed.append(
                    pltpu.make_async_copy(
                        held.at[slot, pl.ds(low, share), :],
                        target.at[block, pl.ds(offset + number * tile, tile)],
                        sems.at[slot, index],
                    )
                )
            return listed

        for number in range(tiles):

            @pl.when(step == number)
            def _():
                if number >= 2:
                    for copy in copies(number - 2):
                        copy.wait()
                held[number % 2] = dot_tn(left_ref[...], right_ref[...]).astype(bf16)
                for copy in copies(number):
                    copy.start()
                if number == tiles - 1:
                    for past in range(max(tiles - 2, 0), tiles):
                        for copy in copies(past):
                            copy.wait()

    return pl.pallas_call(
        ordered(kernel, len(after)),
        grid=(tiles,),
        in_specs=unread(after)
        + [
            whole(left.shape),
            pl.BlockSpec((tokens, tile), lambda i: (0, i + column * tiles)),
            pl.BlockSpec(memory_space=pltpu.SMEM),
        ]
        + unread(into),
        input_output_aliases={len(after) + 3 + index: index for index in range(len(into))},
        out_specs=[pl.BlockSpec(memory_space=pl.ANY)] * 2,
        out_shape=[jax.ShapeDtypeStruct((D // 2, whole_width), bf16)] * 2,
        scratch_shapes=[
            pltpu.VMEM((2, D, tile), bf16),
            pltpu.SemaphoreType.DMA((2, len(masks))),
        ],
        compiler_params=pltpu.CompilerParams(vmem_limit_bytes=vmem_bytes),
        cost_estimate=estimate(
            flops=2 * tokens * D * width,
            bytes_accessed=2 * (D + tokens) * width + 2 * tokens * D,
            transcendentals=0,
        ),
        name="masked_grads",
    )(*after, left, right, place[0], *into)


def third_grads(hidden, ffn_back, place, total, offset, after=()):
    tokens, length = hidden.shape
    width = D // 3
    masks = place[1]
    count = len(masks[0])
    share = length // count
    half = count // 2

    def kernel(left_ref, right_ref, me_ref, *rest):
        targets, held, sems = rest[:6], rest[6], rest[7]
        step = pl.program_id(0)

        def copies(part):
            listed = []
            for index, mask in enumerate(masks[part]):
                low = pl.multiple_of((me_ref[0] ^ mask) * share, share)
                listed.append(
                    pltpu.make_async_copy(
                        held.at[part, pl.ds(low, share), :],
                        targets[2 * part + index // half].at[
                            pl.ds(index % half * share, share), pl.ds(offset, width)
                        ],
                        sems.at[part, index],
                    )
                )
            return listed

        for part in range(3):

            @pl.when(step == part)
            def _():
                held[part] = dot_tn(left_ref[...], right_ref[...]).astype(bf16)
                for copy in copies(part):
                    copy.start()
                if part == 2:
                    for past in range(3):
                        for copy in copies(past):
                            copy.wait()

    results = pl.pallas_call(
        ordered(kernel, len(after)),
        grid=(3,),
        in_specs=unread(after)
        + [
            whole(hidden.shape),
            pl.BlockSpec((tokens, width), lambda i: (0, i)),
            pl.BlockSpec(memory_space=pltpu.SMEM),
        ],
        out_specs=[pl.BlockSpec(memory_space=pl.ANY)] * 6,
        out_shape=[jax.ShapeDtypeStruct((length // 2, total), bf16)] * 6,
        scratch_shapes=[
            pltpu.VMEM((3, length, width), bf16),
            pltpu.SemaphoreType.DMA((3, count)),
        ],
        compiler_params=pltpu.CompilerParams(vmem_limit_bytes=vmem_bytes),
        cost_estimate=estimate(
            flops=2 * tokens * D * length,
            bytes_accessed=2 * (tokens + D) * length + 2 * tokens * D,
            transcendentals=0,
        ),
        name="third_grads",
    )(*after, hidden, ffn_back, place[0])
    return [(results[2 * part], results[2 * part + 1]) for part in range(3)]


def head_lanes(shape, axis, head):
    lane = lax.broadcasted_iota(jnp.int32, shape, axis)
    return (lane >= HD) == (head == 1)


def attend(queries, keys, values, spec_of, width, query_image, key_image):
    length = queries.shape[0]
    pairs = width // LANES
    part = min(1024, length)

    def kernel(q_ref, k_ref, v_ref, qi_ref, ki_ref, out_ref, log_ref):
        key_block = k_ref[...]
        value_turned = v_ref[...].T
        key_parts = []
        value_parts = []
        for head in range(2):
            mine = head_lanes((length, LANES), 1, head)
            key_parts.append(jnp.where(mine, key_block, ki_ref[...]))
            value_parts.append(
                jnp.where(head_lanes((LANES, length), 0, head), value_turned, jnp.ones((), bf16))
            )

        for low in range(0, length, part):
            rows = pl.ds(low, part)
            query = q_ref[rows, :] * jnp.asarray(HD ** (-0.5), bf16)
            scores = []
            for head in range(2):
                mine = head_lanes((part, LANES), 1, head)
                scores.append(
                    dot_nt(key_parts[head], jnp.where(mine, query, qi_ref[rows, :]))
                )
            tops = [jnp.max(score, axis=0, keepdims=True) for score in scores]
            raised = [jnp.exp(score - top).astype(bf16) for score, top in zip(scores, tops)]
            results = [dot_nn(value_parts[head], raised[head]) for head in range(2)]
            turned = []
            for head in range(2):
                lane = HD * (1 - head)
                count = results[head][lane : lane + 1, :]
                turned.append(results[head][head * HD : (head + 1) * HD, :] / count)
                log_ref[0, pl.ds(head, 1), rows] = tops[head] + jnp.log(count)
            out_ref[rows, :] = jnp.concatenate(turned, axis=0).T.astype(bf16)

    return pl.pallas_call(
        kernel,
        grid=(pairs,),
        in_specs=[
            pl.BlockSpec((length, LANES), spec_of(0)),
            pl.BlockSpec((length, LANES), spec_of(1)),
            pl.BlockSpec((length, LANES), spec_of(2)),
            whole(query_image.shape),
            whole(key_image.shape),
        ],
        out_specs=[
            pl.BlockSpec((length, LANES), lambda i: (0, i)),
            pl.BlockSpec((1, 2, length), lambda i: (i, 0, 0)),
        ],
        out_shape=[
            jax.ShapeDtypeStruct((length, width), bf16),
            jax.ShapeDtypeStruct((pairs, 2, length), f32),
        ],
        compiler_params=pltpu.CompilerParams(vmem_limit_bytes=vmem_bytes),
        cost_estimate=estimate(
            flops=16 * pairs * length * length * HD * 4,
            bytes_accessed=8 * length * width,
            transcendentals=2 * pairs * length * length,
        ),
        name="attend",
    )(queries, keys, values, query_image, key_image)


def attend_back(
    queries, keys, values, spec_of, width, attended, grads, log_total, query_image, key_image,
    pairs, first, before, after=(),
):
    length = queries.shape[0]
    part = min(1024, length)
    score_scale = HD ** (-0.5)

    def kernel(
        q_ref, k_ref, v_ref, o_ref, g_ref, log_ref, qi_ref, ki_ref, *rest
    ):
        dq_ref, dk_ref, dv_ref, key_sum, value_sum = rest[-5:]
        key_block = k_ref[...]
        value_block = v_ref[...]
        key_turned = key_block.T
        key_parts = []
        value_parts = []
        for head in range(2):
            mine = head_lanes((length, LANES), 1, head)
            key_parts.append(jnp.where(mine, key_block, ki_ref[...]))
            value_parts.append(jnp.where(mine, value_block, jnp.zeros((), bf16)))
        key_sum[...] = jnp.zeros_like(key_sum)
        value_sum[...] = jnp.zeros_like(value_sum)
        sel_rows = lax.broadcasted_iota(jnp.int32, (8, LANES), 0)
        sel_lanes = lax.broadcasted_iota(jnp.int32, (8, LANES), 1)
        select = jnp.where(
            sel_rows == jnp.where(sel_lanes >= HD, 1, 0), jnp.ones((), f32), jnp.zeros((), f32)
        ).astype(bf16)

        for low in range(0, length, part):
            rows = pl.ds(low, part)
            query = q_ref[rows, :] * jnp.asarray(score_scale, bf16)
            grad = g_ref[rows, :]
            product = grad.astype(f32) * o_ref[rows, :].astype(f32)
            upper = product.astype(bf16)
            lower = (product - upper.astype(f32)).astype(bf16)
            inner = dot_nt(select, upper) + dot_nt(select, lower)
            turned = []
            for head in range(2):
                mine = head_lanes((part, LANES), 1, head)
                scores = dot_nt(key_parts[head], jnp.where(mine, query, qi_ref[rows, :]))
                chances = jnp.exp(scores - log_ref[0, pl.ds(head, 1), rows])
                grad_chances = dot_nt(value_parts[head], grad)
                grad_scores = (chances * (grad_chances - inner[head : head + 1, :])).astype(bf16)
                value_sum[head] += dot_nn(chances.astype(bf16), grad)
                key_sum[head] += dot_nn(grad_scores, query)
                result = dot_nn(key_turned, grad_scores)
                turned.append(result[head * HD : (head + 1) * HD, :])
            dq_ref[rows, :] = (jnp.concatenate(turned, axis=0).T * score_scale).astype(bf16)
        lower_lanes = head_lanes((length, LANES), 1, 0)
        dk_ref[...] = jnp.where(lower_lanes, key_sum[0], key_sum[1]).astype(bf16)
        dv_ref[...] = jnp.where(lower_lanes, value_sum[0], value_sum[1]).astype(bf16)

    column = pl.BlockSpec((length, LANES), lambda i: (0, i + first))
    moved = lambda which: (lambda i: spec_of(which)(i + first))
    held = list(before or [])
    return pl.pallas_call(
        ordered(kernel, len(after)),
        grid=(pairs,),
        in_specs=unread(after)
        + [
            pl.BlockSpec((length, LANES), moved(0)),
            pl.BlockSpec((length, LANES), moved(1)),
            pl.BlockSpec((length, LANES), moved(2)),
            column,
            column,
            pl.BlockSpec((1, 2, length), lambda i: (i + first, 0, 0)),
            whole(query_image.shape),
            whole(key_image.shape),
        ]
        + [pl.BlockSpec(memory_space=pl.ANY)] * len(held),
        input_output_aliases={len(after) + 8 + index: index for index in range(len(held))},
        out_specs=[column] * 3,
        out_shape=[jax.ShapeDtypeStruct((length, width), bf16)] * 3,
        scratch_shapes=[
            pltpu.VMEM((2, length, LANES), f32),
            pltpu.VMEM((2, length, LANES), f32),
        ],
        compiler_params=pltpu.CompilerParams(vmem_limit_bytes=vmem_bytes),
        cost_estimate=estimate(
            flops=40 * pairs * length * length * HD * 4,
            bytes_accessed=16 * length * width,
            transcendentals=2 * pairs * length * length,
        ),
        name="attend_back",
    )(*after, queries, keys, values, attended, grads, log_total, query_image, key_image, *held)


def gate_up_rows(normed, weight):
    tokens = normed.shape[0]
    tile = 512
    tiles = FF // tile

    def kernel(left_ref, gate_weight, up_weight, hidden_ref, gate_ref, up_ref):
        gate = dot_nn(left_ref[...], gate_weight[...])
        up = dot_nn(left_ref[...], up_weight[...])
        hidden_ref[...] = (gate / (1.0 + jnp.exp(-gate)) * up).astype(bf16)
        gate_ref[...] = gate.astype(bf16)
        up_ref[...] = up.astype(bf16)

    out = pl.BlockSpec((tokens, tile), lambda i: (0, i))
    return pl.pallas_call(
        kernel,
        grid=(tiles,),
        in_specs=[
            whole(normed.shape),
            pl.BlockSpec((D, tile), lambda i: (0, i)),
            pl.BlockSpec((D, tile), lambda i: (0, i + tiles)),
        ],
        out_specs=[out] * 3,
        out_shape=[jax.ShapeDtypeStruct((tokens, FF), bf16)] * 3,
        compiler_params=pltpu.CompilerParams(vmem_limit_bytes=vmem_bytes),
        cost_estimate=estimate(
            flops=4 * tokens * D * FF, bytes_accessed=4 * D * FF + 6 * tokens * FF, transcendentals=0
        ),
        name="gate_up_rows",
    )(normed, weight, weight)


def gate_up_back(ffn_back, weight, gate, up, after=()):
    tokens = ffn_back.shape[0]
    tile = 512
    tiles = FF // tile

    def kernel(left_ref, weight_ref, gate_ref, up_ref, gate_back, up_back):
        grad = dot_nt(left_ref[...], weight_ref[...])
        gate_rows = gate_ref[...].astype(f32)
        share = 1.0 / (1.0 + jnp.exp(-gate_rows))
        active = gate_rows * share
        up_back[...] = (grad * active).astype(bf16)
        slope = share + active * (1.0 - share)
        gate_back[...] = (grad * up_ref[...].astype(f32) * slope).astype(bf16)

    column = pl.BlockSpec((tokens, tile), lambda i: (0, i))
    return pl.pallas_call(
        ordered(kernel, len(after)),
        grid=(tiles,),
        in_specs=unread(after)
        + [
            whole(ffn_back.shape),
            pl.BlockSpec((tile, D), lambda i: (i, 0)),
            column,
            column,
        ],
        out_specs=[column] * 2,
        out_shape=[jax.ShapeDtypeStruct((tokens, FF), bf16)] * 2,
        compiler_params=pltpu.CompilerParams(vmem_limit_bytes=vmem_bytes),
        cost_estimate=estimate(
            flops=2 * tokens * D * FF, bytes_accessed=2 * D * FF + 8 * tokens * FF, transcendentals=0
        ),
        name="gate_up_back",
    )(*after, ffn_back, weight, gate, up)


def output_rows(attended, weight, column, embedded, image, post_table, pre_table):
    def body(value, rows, ins, consts, outs, scratch):
        hat = value * inverse_rms(value)
        image_rows = ins[1][rows, :1]
        mixed = ins[0][rows, :] + picked(image_rows, consts[0][...]) * hat
        outs[0][rows, :] = value
        outs[1][rows, :] = mixed
        outs[2][rows, :] = (
            mixed * inverse_rms(mixed) * picked(image_rows, consts[1][...])
        ).astype(bf16)

    return matmul_rows(
        "output_rows", [attended], weight, "nn", 768, [embedded, image], [post_table, pre_table],
        [(D, f32), (D, f32), (D, bf16)], [], body, shape=(D, D), column=column,
    )


def down_rows(hidden, weight, mixed, image, onehot, grad_patches, post_table, out_table, w_final):
    def before(ins, consts, outs, scratch):
        scratch[0][...] = dot_nt(ins[3][...], consts[2][...])

    def body(value, rows, ins, consts, outs, scratch):
        inverse = inverse_rms(value)
        hat = value * inverse
        image_rows = ins[1][rows, :1]
        post = picked(image_rows, consts[0][...])
        final_state = ins[0][rows, :] + post * hat
        centred = final_state - row_mean(final_state)
        spread = inverse_rms(centred)
        levelled = centred * spread
        scale = picked(image_rows, consts[1][...])
        outs[0][rows, :] = (levelled * scale).astype(bf16)
        grad = scratch[0][rows, :]
        scratch[1][rows, :] = grad * levelled
        back = grad * scale
        late = spread * (back - row_mean(back) - levelled * row_mean(back * levelled))
        outs[1][rows, :] = late
        scratch[2][rows, :] = late * hat
        back = late * post
        outs[2][rows, :] = (inverse * (back - hat * row_mean(back * hat))).astype(bf16)

    def after(ins, consts, outs, sums, scratch):
        outs[3][...] = dot_nn(outs[0][...], consts[2][...]).astype(bf16)
        one = ins[2][...]
        sums[0][...] += image_sums(one, scratch[1][...])
        sums[1][...] += image_sums(one, scratch[2][...])

    return matmul_rows(
        "down_rows", [hidden], weight, "nn", 1024, [mixed, image, onehot, grad_patches],
        [post_table, out_table, w_final],
        [(D, bf16), (D, f32), (D, bf16), (PIN, bf16)], [8, 8], body,
        before=before, after=after, block_scratch=[(D, f32)] * 3,
    )


def ffn_back_rows(
    gate_back, up_back, weight, late, mixed, attn_out, image, onehot, post_table, pre_table,
    wait=(),
):
    def body(value, rows, ins, consts, outs, scratch):
        image_rows = ins[3][rows, :1]
        mixed_rows = ins[1][rows, :]
        inverse = inverse_rms(mixed_rows)
        hat = mixed_rows * inverse
        scratch[0][rows, :] = value * hat
        back = value * picked(image_rows, consts[1][...])
        early = ins[0][rows, :] + inverse * (back - hat * row_mean(back * hat))
        outs[0][rows, :] = early
        attn_rows = ins[2][rows, :]
        inverse = inverse_rms(attn_rows)
        hat = attn_rows * inverse
        scratch[1][rows, :] = early * hat
        back = early * picked(image_rows, consts[0][...])
        outs[1][rows, :] = (inverse * (back - hat * row_mean(back * hat))).astype(bf16)

    def after(ins, consts, outs, sums, scratch):
        one = ins[4][...]
        sums[0][...] += image_sums(one, scratch[0][...])
        sums[1][...] += image_sums(one, scratch[1][...])

    return matmul_rows(
        "ffn_back_rows", [gate_back, up_back], weight, "nt", 1024,
        [late, mixed, attn_out, image, onehot], [post_table, pre_table],
        [(D, f32), (D, bf16)], [8, 8], body, after=after, block_scratch=[(D, f32)] * 2,
        wait=wait,
    )


def project_back_rows(
    backs, weight, embedded, late, image, onehot, pre_table, w_embed, wait=()
):
    def body(value, rows, ins, consts, outs, scratch):
        embedded_rows = ins[0][rows, :]
        inverse = inverse_rms(embedded_rows)
        hat = embedded_rows * inverse
        scratch[0][rows, :] = value * hat
        back = value * picked(ins[2][rows, :1], consts[0][...])
        early = inverse * (back - hat * row_mean(back * hat))
        outs[0][rows, :] = (early + ins[1][rows, :]).astype(bf16)

    def after(ins, consts, outs, sums, scratch):
        outs[1][...] = dot_nn(outs[0][...], consts[1][...]).astype(bf16)
        sums[0][...] += image_sums(ins[3][...], scratch[0][...])

    return matmul_rows(
        "project_back_rows", backs, weight, "nt", D,
        [embedded, late, image, onehot], [pre_table, w_embed],
        [(D, bf16), (PIN, bf16)], [8], body, after=after, block_scratch=[(D, f32)], wait=wait,
        shape=(3 * D, D),
    )


def turn_back(grad_q, grad_k, hats, inverses, cosine, sine, gains, after=()):
    tokens = grad_q.shape[0]
    block = min(256, tokens)
    chunk = 64

    def kernel(gq_ref, gk_ref, hat_ref, inv_ref, cos_ref, sin_ref, gain_ref, out_ref, sum_ref):
        @pl.when(pl.program_id(0) == 0)
        def _():
            sum_ref[...] = jnp.zeros_like(sum_ref)

        for which, grad_ref in enumerate((gq_ref, gk_ref)):
            gain = gain_ref[which : which + 1, :]

            total = jnp.zeros((8, D), f32)
            for low in range(0, block, chunk):
                rows = pl.ds(low, chunk)
                first = first_lanes(chunk)
                cos_rows = cos_ref[rows, :]
                sin_rows = sin_ref[rows, :]
                pieces = []
                for lane in range(0, D, LANES):
                    part = grad_ref[rows, lane : lane + LANES].astype(f32)
                    pieces.append(part * cos_rows - swapped(part, first) * sin_rows)
                turned = jnp.concatenate(pieces, axis=1)
                hat = hat_ref[rows, which * D : (which + 1) * D].astype(f32)
                inverse = inv_ref[rows, which * LANES : which * LANES + 1]
                back = turned * gain
                out_ref[rows, which * D : (which + 1) * D] = (
                    inverse * (back - hat * row_mean(back * hat))
                ).astype(bf16)
                total = total + jnp.sum((turned * hat).reshape(chunk // 8, 8, D), axis=0)
            sum_ref[which : which + 1, :] += jnp.sum(total, axis=0, keepdims=True)

    row = lambda cols: pl.BlockSpec((block, cols), lambda i: (i, 0))
    return pl.pallas_call(
        ordered(kernel, len(after)),
        grid=(tokens // block,),
        in_specs=unread(after)
        + [
            row(D), row(D), row(2 * D), row(2 * LANES), row(LANES), row(LANES), whole(gains.shape)
        ],
        out_specs=[row(2 * D), pl.BlockSpec((8, D), lambda i: (0, 0))],
        out_shape=[
            jax.ShapeDtypeStruct((tokens, 2 * D), bf16),
            jax.ShapeDtypeStruct((8, D), f32),
        ],
        compiler_params=pltpu.CompilerParams(vmem_limit_bytes=vmem_bytes),
        cost_estimate=estimate(
            flops=40 * tokens * D, bytes_accessed=12 * tokens * D, transcendentals=0
        ),
        name="turn_back",
    )(*after, grad_q, grad_k, hats, inverses, cosine, sine, gains)


def to_strips(tiles):
    micros = tiles.shape[0]
    count = lax.axis_size("rows")
    parts = count // micros
    me = lax.axis_index("rows")
    slots = []
    for shift in range(micros):
        pairs = [(q, ((q % micros - shift) % micros) * parts + q // micros) for q in range(count)]
        sent = lax.dynamic_index_in_dim(tiles, (me % micros - shift) % micros, 0, keepdims=False)
        if any(a != b for a, b in pairs):
            sent = lax.ppermute(sent, "rows", pairs)
        slots.append(sent)
    stacked = jnp.stack(slots)
    order = (jnp.arange(micros) - me // parts) % micros
    ordered = jnp.concatenate(
        [lax.dynamic_index_in_dim(stacked, order[d], 0) for d in range(micros)], axis=0
    )
    kinds, height, width = ordered.shape[1:]
    return ordered.transpose(1, 0, 2, 3).reshape(kinds, micros * height, width)


def from_strips(strip, micros):
    count = lax.axis_size("rows")
    parts = count // micros
    me = lax.axis_index("rows")
    kinds, height, width = strip.shape
    tiles = strip.reshape(kinds, micros, height // micros, width).transpose(1, 0, 2, 3)
    slots = []
    for shift in range(micros):
        pairs = [(((q % micros - shift) % micros) * parts + q // micros, q) for q in range(count)]
        sent = lax.dynamic_index_in_dim(tiles, (me // parts + shift) % micros, 0, keepdims=False)
        if any(a != b for a, b in pairs):
            sent = lax.ppermute(sent, "rows", pairs)
        slots.append(sent)
    stacked = jnp.stack(slots)
    return jnp.concatenate(
        [
            lax.dynamic_index_in_dim(stacked, (me % micros - m) % micros, 0)
            for m in range(micros)
        ],
        axis=0,
    )


def neighbour_pairs(axis, parts):
    count = lax.axis_size(axis)
    ups = [(i, i + 1) for i in range(count - 1) if (i + 1) % parts != 0]
    return ups, [(b, a) for a, b in ups]


def neighbours(values, axis, dim, parts):
    ups, downs = neighbour_pairs(axis, parts)
    head = lax.slice_in_dim(values, 0, 1, axis=dim)
    tail = lax.slice_in_dim(values, values.shape[dim] - 1, values.shape[dim], axis=dim)
    if len(ups) == 0:
        return jnp.zeros_like(head), jnp.zeros_like(tail)
    return lax.ppermute(tail, axis, ups), lax.ppermute(head, axis, downs)


def sides(parts):
    return (("cols", 1, lax.axis_size("cols")), ("rows", 0, parts))


def window_filter(turned):
    values = jnp.eye(PIN, dtype=bf16).reshape(PIN, CHANNELS, 4, 4)
    return values[:, :, ::-1, ::-1].transpose(1, 0, 2, 3) if turned else values


def extract_patches(strip, parts):
    for axis, dim, span in sides(parts):
        before, after = neighbours(strip, axis, dim + 1, span)
        strip = jnp.concatenate([before, strip, after], axis=dim + 1)
    kinds, height, width = strip.shape
    sets = kinds // CHANNELS
    rows, cols = height // 2 - 1, width // 2 - 1
    windows = lax.conv_general_dilated(
        strip.reshape(sets, CHANNELS, height, width),
        window_filter(False),
        (2, 2),
        "VALID",
        dimension_numbers=("NCHW", "OIHW", "NHWC"),
        preferred_element_type=f32,
    )
    return windows.astype(bf16).reshape(sets, rows * cols, PIN)


def fold_patches(pieces, rows, cols):
    canvas = lax.conv_general_dilated(
        pieces.reshape(1, rows, cols, PIN),
        window_filter(True),
        (1, 1),
        ((3, 3), (3, 3)),
        lhs_dilation=(2, 2),
        dimension_numbers=("NHWC", "OIHW", "NCHW"),
        preferred_element_type=f32,
    )
    return canvas[0]


def share_rims(canvas, parts):
    for axis, dim, span in sides(parts):
        dim += 1
        before, after = neighbours(canvas, axis, dim, span)
        size = canvas.shape[dim]
        middle = list(canvas.shape)
        middle[dim] = size - 4
        canvas = lax.slice_in_dim(canvas, 1, size - 1, axis=dim)
        canvas = canvas + jnp.concatenate([before, jnp.zeros(middle, f32), after], axis=dim)
    return canvas


def strip_layout(heights, seq_rows):
    starts = jnp.cumsum(heights) - heights
    rows_all = jnp.arange(seq_rows, dtype=jnp.int32)
    image_of = jnp.sum((rows_all[:, None] >= starts[None, 1:]).astype(jnp.int32), axis=1)
    start_of = jnp.sum(
        jnp.where(
            image_of[:, None] == jnp.arange(IMGS, dtype=jnp.int32)[None, :], starts[None, :], 0
        ),
        axis=1,
    )
    return (image_of, rows_all - start_of)


def rope_tables(row_place, column):
    quarter = HD // 4
    lane = jnp.arange(LANES, dtype=jnp.int32)
    frequency = 10000.0 ** (-(lane % quarter).astype(f32) / quarter)
    spot = jnp.where((lane % HD < HD // 2)[None, :], row_place[:, None], column[:, None])
    angles = spot.astype(f32) * frequency[None, :]
    sign = jnp.where(lane % 32 < 16, -1.0, 1.0)
    return (jnp.cos(angles), jnp.sin(angles) * sign[None, :])


def gather_all(shard):
    return lax.all_gather(shard, ALL, axis=0, tiled=True)


def scatter_all(part):
    return lax.psum_scatter(part, ALL, scatter_dimension=0, tiled=True)


def bits_of(axis):
    return lax.axis_size(axis).bit_length() - 1


def orders():
    first = [("fsdp", bit) for bit in range(bits_of("fsdp"))]
    main = [("cols", 0), ("rows", 0), ("cols", 1)]
    rest = [("rows", bit) for bit in range(1, bits_of("rows"))]
    rest += [("cols", bit) for bit in range(2, bits_of("cols"))]
    return [first + main[turn:] + main[:turn] + rest for turn in range(3)]


def block_masks(order):
    base = {"fsdp": 0, "cols": bits_of("fsdp"), "rows": bits_of("fsdp") + bits_of("cols")}
    steps = len(order)
    return [
        sum(
            ((index >> (steps - 1 - step)) & 1) << (base[axis] + bit)
            for step, (axis, bit) in enumerate(order)
        )
        for index in range(1 << steps)
    ]


def swap(values, axis, bit):
    return lax.ppermute(values, axis, [(i, i ^ (1 << bit)) for i in range(lax.axis_size(axis))])


class Gather:
    def __init__(self, values, picks):
        self.steps = [list(reversed(order)) for order in picks]
        self.held = list(values)
        self.step = 0
        self.received = []

    def start(self):
        self.received = [
            swap(value, *self.steps[k][self.step]) for k, value in enumerate(self.held)
        ]

    def finish(self):
        self.step += 1
        if self.done():
            self.held = list(zip(self.held, self.received))
        else:
            self.held = [jnp.concatenate(pair, axis=0) for pair in zip(self.held, self.received)]

    def done(self):
        return self.step == len(self.steps[0])


class Scatter:
    def __init__(self, halves, picks):
        self.steps = picks
        self.terms = [[kept] for kept, _ in halves]
        self.sent = [sent for _, sent in halves]
        self.kinds = [kept.dtype for kept, _ in halves]
        self.step = 0
        self.received = []

    def total(self, values):
        return sum(value.astype(f32) for value in values)

    def sent_next(self):
        sent = []
        for terms, kind in zip(self.terms, self.kinds):
            half = terms[0].shape[0] // 2
            sent.append(self.total([term[half:] for term in terms]).astype(kind))
        return sent

    def start(self):
        if self.step > 0:
            self.sent = self.sent_next()
            self.terms = [[term[: term.shape[0] // 2] for term in terms] for terms in self.terms]
        self.received = [
            swap(sent, *order[self.step]) for sent, order in zip(self.sent, self.steps)
        ]

    def finish(self):
        self.step += 1
        self.terms = [terms + [value] for terms, value in zip(self.terms, self.received)]

    def done(self):
        return self.step == len(self.steps[0])

    def sums(self):
        return [self.total(values) for values in self.terms]


def halves_of(values):
    half = values.shape[0] // 2
    return values[:half], values[half:]


def wait_for(chain, *others):
    chain.received[0] = held_until(chain.received[0], *others)


def step_all(value, *chains):
    for chain in chains:
        wait_for(chain, value)
    go_on(*chains)


def arrived(*chains):
    return tuple(value for chain in chains for value in chain.received)


def go_on(*chains):
    for chain in chains:
        chain.finish()
        if not chain.done():
            chain.start()


def exchange_heads(parts, micros):
    groups = [[m * parts + s for s in range(parts)] for m in range(micros)]

    def spread(values):
        return lax.all_to_all(
            values, "rows", split_axis=1, concat_axis=0, tiled=True, axis_index_groups=groups
        )

    def collect(values):
        return lax.all_to_all(
            values, "rows", split_axis=0, concat_axis=1, tiled=True, axis_index_groups=groups
        )

    return spread, collect


def shards(
    latent,
    time_embed,
    image_rows,
    pred_grad,
    embed_weight,
    adaptive_weight,
    project_weight,
    output_weight,
    gate_up_weight,
    down_weight,
    final_weight,
    norm_gains,
):
    micros = latent.shape[0]
    row_devices = lax.axis_size("rows")
    parts = row_devices // micros
    row_index = lax.axis_index("rows")
    micro, piece = row_index // parts, row_index % parts
    device = (row_index * lax.axis_size("cols") + lax.axis_index("cols")) * lax.axis_size(
        "fsdp"
    ) + lax.axis_index("fsdp")
    rows = latent.shape[3] // 2 * micros
    cols = latent.shape[4] // 2
    tokens = rows * cols
    seq_rows = rows * parts
    length = seq_rows * cols

    devices = lax.axis_size(ALL)
    share = D // devices
    near = share % 16 == 0 and FF // devices % LANES == 0
    picks = orders()
    place = None
    if near:
        place = (device.astype(jnp.int32).reshape(1), [block_masks(order) for order in picks])

    tiles = jnp.concatenate([latent[:, 0], pred_grad[:, 0]], axis=1)
    small = jnp.concatenate(
        [
            embed_weight,
            final_weight,
            norm_gains,
            jnp.zeros((norm_gains.shape[0], 2 * LANES - 2 * PIN - 6), bf16),
        ],
        axis=1,
    )
    temb = lax.dynamic_index_in_dim(time_embed, micro, 0, keepdims=False)[0, 0]
    condition = jax.nn.silu(temb).astype(bf16)
    rows_held = adaptive_weight.shape[0]
    if near:
        wide = condition.reshape(-1, 2 * LANES)
        side = Gather([jnp.concatenate([small, wide], axis=0)], picks[:1])
        side.start()
        while not side.done():
            go_on(side)
        small_pairs = side.held
        both = jnp.concatenate(side.held[0], axis=0)
        both = both.reshape(devices, share + wide.shape[0], 2 * LANES)
        conditions = both[:, share:].reshape(devices * IMGS, condition.shape[1])
        conditions = lax.dynamic_slice_in_dim(conditions, device * rows_held, rows_held, axis=1)
        per_image = dot_nn(conditions, adaptive_weight)
        side = Scatter([halves_of(per_image)], picks[:1])
        side.start()
        while not side.done():
            go_on(side)
        joined = gather_all(jnp.concatenate([project_weight, output_weight], axis=1))
        w_project = joined
        w_output = joined[:, 3 * D :]
        w_down = gather_all(down_weight)
        per_image = side.sums()[0]
        source = jnp.asarray(place[1][0], jnp.int32)
        count = len(picks[0])
        small = arrange(small_pairs, place, share)
    else:
        small = gather_all(small)
        conditions = gather_all(condition)
        conditions = lax.dynamic_slice_in_dim(conditions, device * rows_held, rows_held, axis=1)
        per_image = scatter_all(dot_nn(conditions, adaptive_weight))
        w_project = gather_all(project_weight)
        w_output = gather_all(output_weight)
        joined = w_output
        w_down = gather_all(down_weight)
    w_embed = small[:, :PIN]
    w_final = small[:, PIN : 2 * PIN]
    gains = small[:, 2 * PIN : 2 * PIN + 6].astype(f32).T

    w_gate_up = gather_all(gate_up_weight)

    patches, grad_patches = extract_patches(to_strips(tiles), parts)

    heights = lax.dynamic_index_in_dim(image_rows, micro, 0, keepdims=False)[0, 0]
    row_image, row_place = strip_layout(heights, seq_rows)
    first_row = piece * rows
    my_image = lax.dynamic_slice_in_dim(row_image, first_row, rows)
    my_place = lax.dynamic_slice_in_dim(row_place, first_row, rows)
    token_image = jnp.repeat(my_image, cols)
    cosine, sine = rope_tables(
        jnp.repeat(my_place, cols), jnp.tile(jnp.arange(cols, dtype=jnp.int32), rows)
    )
    image = jnp.broadcast_to(token_image[:, None], (tokens, LANES))
    onehot = (token_image[None, :] == jnp.arange(8, dtype=jnp.int32)[:, None]).astype(bf16)
    strip_image = jnp.repeat(row_image, cols)
    head_lane = jnp.arange(LANES, dtype=jnp.int32)[None, :] % HD
    same = strip_image[:, None] == head_lane
    query_image = jnp.where(same, -mask_level, 0.0).astype(bf16)
    key_image = jnp.where(same | (head_lane >= IMGS), 0.0, mask_level).astype(bf16)

    modulation = per_image.reshape(IMGS, 5, D)
    scale_attn = 1.0 + modulation[:, 0]
    gate_attn = jnp.tanh(modulation[:, 1])
    scale_ffn = 1.0 + modulation[:, 2]
    gate_ffn = jnp.tanh(modulation[:, 3])
    scale_out = 1.0 + modulation[:, 4]
    table = lambda values: jnp.concatenate([values, values], axis=0)
    attn_pre = table(scale_attn * gains[0])
    attn_post = table(gate_attn * gains[3])
    ffn_pre = table(scale_ffn * gains[4])
    ffn_post = table(gate_ffn * gains[5])
    out_scale = table(scale_out)
    turn_gains = jnp.concatenate([gains[1:3], jnp.zeros((6, D), f32)], axis=0)
    factors = [
        jnp.broadcast_to(gains[0], (IMGS, D)),
        (1.0 - gate_attn * gate_attn) * gains[3],
        jnp.broadcast_to(gains[4], (IMGS, D)),
        (1.0 - gate_ffn * gate_ffn) * gains[5],
        jnp.ones((IMGS, D), f32),
    ]

    embedded, normed, projected, hats, inverses = project_rows(
        patches, image, cosine, sine, w_embed, attn_pre, w_project, turn_gains
    )
    if parts == 1:
        pairs = D // LANES
        heads = (projected, projected, projected)
        spec_of = lambda which: (lambda i: (0, which * pairs + i))
        width = D
    else:
        spread, collect = exchange_heads(parts, micros)
        heads = tuple(spread(projected[:, w * D : (w + 1) * D]) for w in range(3))
        spec_of = lambda which: (lambda i: (0, i))
        width = D // parts
    attended_heads, log_total = attend(*heads, spec_of, width, query_image, key_image)
    attended = attended_heads if parts == 1 else collect(attended_heads)
    attn_out, mixed, normed_ffn = output_rows(
        attended, joined, 3 if near else 0, embedded, image, attn_post, ffn_pre
    )
    hidden, gate, up = gate_up_rows(normed_ffn, w_gate_up)
    final, late, ffn_back, pieces, sum_out, sum_ffn_post = down_rows(
        hidden, w_down, mixed, image, onehot, grad_patches, ffn_post, out_scale, w_final
    )
    if near:
        down_parts = third_grads(hidden, ffn_back, place, D // 3, 0)
        down_chain = Scatter(down_parts, picks)
        down_chain.start()
        gate_back, up_back = gate_up_back(
            ffn_back, w_down, gate, up, after=[part[0] for part in down_parts]
        )
        waits = arrived(down_chain)
        step_all(gate_back, down_chain)
        waits += tuple(down_chain.sent)
        gate_up_grad = gate_up_grads(normed_ffn, gate_back, up_back, after=waits)
        gate_up_share = scatter_all(gate_up_grad)
        waits = (gate_up_grad,)
    else:
        down_share = scatter_all(dot_tn(hidden, ffn_back).astype(bf16))
        gate_back, up_back = gate_up_back(ffn_back, w_down, gate, up)
        gate_up_share = scatter_all(gate_up_grads(normed_ffn, gate_back, up_back))
        waits = ()
    early, attn_back, sum_ffn_pre, sum_attn_post = ffn_back_rows(
        gate_back, up_back, w_gate_up, late, mixed, attn_out, image, onehot, attn_post, ffn_pre,
        wait=waits,
    )
    grad_attended = dot_nt(attn_back, w_output).astype(bf16)
    if parts > 1:
        grad_attended = spread(grad_attended)
    back = partial(
        attend_back,
        *heads, spec_of, width, attended_heads, grad_attended, log_total, query_image, key_image,
    )
    if near:
        group = width // LANES // 2
        waits = arrived(down_chain)
        step_all(grad_attended, down_chain)
        waits += tuple(down_chain.sent)
        grads = back(width // LANES, 0, None, after=waits)
    else:
        grads = back(width // LANES, 0, None)
    if parts > 1:
        grads = tuple(collect(grad) for grad in grads)
    grad_q, grad_k, grad_v = grads
    waits = ()
    if near:
        waits = arrived(down_chain)
        step_all(grad_q, down_chain)
        waits += tuple(down_chain.sent)
    turned, sum_turn = turn_back(
        grad_q, grad_k, hats, inverses, cosine, sine, turn_gains, after=waits
    )
    waits = ()
    if near:
        side_width = D // 3
        grad_parts = third_grads(
            attended, attn_back, place, D + side_width, D, after=(grads[0],)
        )
        for k, (back_values, column) in enumerate(((turned, 0), (turned, 1), (grad_v, 0))):
            grad_parts[k] = masked_grads(
                normed, back_values, column, D, place, k, D + side_width, 0, into=grad_parts[k]
            )
        main = Scatter(grad_parts, picks)
        main.start()
        pieces = held_until(pieces, grad_parts[1][0])
    folded = fold_patches(pieces, rows, cols)
    if near:
        waits = arrived(down_chain) + tuple(part[0] for part in grad_parts) + (folded,)
        step_all(grad_parts[0][0], down_chain)
        waits += tuple(down_chain.sent)
    embed_back, grad_pieces, sum_attn_pre = project_back_rows(
        [turned, grad_v], w_project, embedded, early, image, onehot, attn_pre, w_embed, wait=waits
    )
    if near:
        while not down_chain.done():
            go_on(down_chain)
        down_share = jnp.concatenate(down_chain.sums(), axis=1)
        if WAIT_FOR_GATE_UP:
            wait_for(main, gate_up_share)
        main.finish()
        first_sent = main.sent_next()
        embed_back = held_until(embed_back, *first_sent[1:])
        sum_attn_pre = held_until(sum_attn_pre, *first_sent[1:])
    gain_grads, grad_modulation = gain_rows(
        [sum_attn_pre, sum_attn_post, sum_ffn_pre, sum_ffn_post, sum_out], factors,
        [scale_attn, gate_attn, scale_ffn, gate_ffn], sum_turn,
    )
    if near:
        side = Scatter(
            [small_grads_near(embed_back, patches, final, grad_patches, gain_grads, place)],
            picks[:1],
        )
        side.start()
        side.finish()
        main.terms[0] = [
            jnp.concatenate([large, tiny.astype(bf16)], axis=1)
            for large, tiny in zip(main.terms[0], side.terms[0])
        ]
        main.start()
        grad_modulation = held_until(grad_modulation, main.received[1])
        spread_sums = Gather([grad_modulation], picks[:1])
        spread_sums.start()
        grad_pieces = held_until(grad_pieces, main.received[1])
        while not main.done():
            go_on(main)
        while not spread_sums.done():
            go_on(spread_sums)
        grad_modulations = jnp.concatenate(spread_sums.held[0], axis=0)
        held = main.sums()
        project_share = jnp.concatenate([value[:, :D] for value in held], axis=1)
        output_share = jnp.concatenate([value[:, D : D + side_width] for value in held], axis=1)
        small_share = held[0][:, D + side_width :]
    else:
        grad_modulations = gather_all(grad_modulation)
        small_grads = jnp.concatenate(
            [dot_tn(embed_back, patches), dot_tn(final, grad_patches), gain_grads.T], axis=1
        )
        small_share = scatter_all(
            jnp.pad(small_grads, ((0, 0), (0, 2 * LANES - small_grads.shape[1])))
        )
        project_back = jnp.concatenate([turned, grad_v], axis=1)
        project_share = scatter_all(dot_tn(normed, project_back).astype(bf16))
        output_share = scatter_all(dot_tn(attended, attn_back).astype(bf16))
    prediction = from_strips(share_rims(folded, parts), micros)
    latent_grad = from_strips(
        share_rims(fold_patches(grad_pieces, rows, cols), parts), micros
    )

    spaced = jnp.pad(
        conditions.reshape(devices, IMGS, rows_held), ((0, 0), (0, IMGS), (0, 0))
    )
    adaptive_share = jnp.concatenate(
        [
            dot_tn(values.reshape(2 * devices * IMGS, rows_held), grad_modulations)
            for values in (spaced, jnp.roll(spaced, IMGS, axis=1))
        ],
        axis=1,
    )
    return (
        prediction[:, None],
        latent_grad[:, None],
        small_share[:, :PIN],
        adaptive_share,
        project_share.astype(f32),
        output_share.astype(f32),
        gate_up_share.astype(f32),
        down_share.astype(f32),
        small_share[:, PIN : 2 * PIN],
        small_share[:, 2 * PIN : 2 * PIN + 6],
    )


def solution(mesh):
    canvas = P(None, "fsdp", None, "rows", "cols")
    weight = P(ALL, None)
    return jax.shard_map(
        shards,
        mesh=mesh,
        in_specs=(canvas, P(None, "fsdp", "cols", None, None), P(None, "fsdp", "cols", None), canvas)
        + (weight,) * 8,
        out_specs=(canvas, canvas) + (weight,) * 8,
        check_vma=False,
    )
```
